512 devices in a mesh: slab: 64 (over x, z_hi, y, core), off: 8 (over z_lo).
Axes of the slice: x: 4, y: 4, z: 16 (z_hi: 2, z_lo: 8; z = z_hi * 8 + z_lo), core: 2. Of those that a mesh axis runs over, the one named last changes fastest.
Arguments:
- bead_data: bfloat16 [524288, 2, 128], P(('slab', 'off')), may hold values from -6 to 6
- bead_cell: int32 [524288], P(('slab', 'off')), may hold values from 0 to 65535, as said below
- m2l_ops: bfloat16 [128, 128, 128], P('off'), may hold values from -0.0625 to 0.0625
- offsets: int32 [128, 3], P('off'), may hold values from -3 to 2, as said below
Outputs:
- bead_field: float32 [524288], P(('slab', 'off'))
The draws below stay inside these ranges and needn't reach their ends.
Inputs may be any that keep to these rules, and one draw needn't show every extreme that they name: `bead_cell`: each device's 1024 beads come in 64 blocks of 16; block s lies in slab s, and is made of 8 runs of 2 beads, run r lying in cells s * 1024 + r * 128 to s * 1024 + (r + 1) * 128 - 1. Distinct offsets whose three components lie in -3 to 2 and are not all in -1 to 1.
All inputs are finite; a program needn't handle non-finite values.
Results may differ from the reference program's by a relative error of at most 0.0029.
Values may be sent and summed in bfloat16 or wider, within the bound.
No kernel may reach another device: no remote copies, remote signals or barrier semaphores. Data moves between devices by JAX's collectives and lax.ppermute only.
A program may use at most 64 MiB of HBM per device.

```python
import jax
import jax.numpy as jnp
import numpy as np
from jax import lax

P_SIZE = 128
GX = 8
GY = 32
CZS = 4
CAP = 16
OFFS = 128
NZ = 256
BEADS = 524288
N_SLAB = 64
N_OFF = 8


def offset_table():
    rows = []
    for dz in range(-3, 3):
        for dx in range(-3, 3):
            for dy in range(-3, 3):
                if max(abs(dz), abs(dx), abs(dy)) > 1:
                    rows.append((dz, dx, dy))
    return np.array(rows, dtype=np.int32)


def draw_offsets(key, part):
    table = jnp.asarray(offset_table())
    order = jax.random.permutation(key, 189)
    return table[order[:OFFS]]


def draw_bead_cell(key, part):
    cells_dev = CZS * GX * GY
    sub_cells = cells_dev // N_OFF
    beads_dev = CAP * N_SLAB
    run_len = CAP // N_OFF
    total = beads_dev * N_SLAB * N_OFF
    rows = jnp.arange(total, dtype=jnp.int32)
    target = rows % beads_dev // CAP
    run_index = rows % CAP // run_len
    inside = jax.random.randint(key, (total,), 0, sub_cells, dtype=jnp.int32)
    return target * cells_dev + run_index * sub_cells + inside


def level_of(rng, extent, split, low, top_value):
    level, own = 1.0, jax.random.fold_in(rng, 6)
    for dim, blocks in split:
        draws = jnp.exp(jax.random.uniform(jax.random.fold_in(own, dim), (blocks,), jnp.float32, low / len(split), top_value / len(split)))
        level = level * jnp.repeat(draws, extent[dim] // blocks).reshape([-1 if axis == dim else 1 for axis in range(len(extent))])
    return level


def scatter_about(stream_key, shape, deviation, limit, cuts=(), kind=jnp.bfloat16):
    values = jax.random.normal(stream_key, shape, jnp.float32) * deviation
    if len(cuts) > 0:
        values = level_of(stream_key, shape, cuts, -0.22, 0.18) * values
    return jnp.clip(values, min=-limit, max=limit).astype(kind)


def setup_inputs(seed: int = 0) -> dict:
    splits = jax.random.split(jax.random.key(seed), 5)
    return {
        "bead_data": scatter_about(splits[0], (BEADS, 2, P_SIZE), 1.0, 6.0, ((0, 512),)),
        "bead_cell": draw_bead_cell(jax.random.fold_in(splits[4], 71), 0),
        "m2l_ops": scatter_about(splits[2], (OFFS, P_SIZE, P_SIZE), (P_SIZE * OFFS // 2) ** -0.5, 0.0625, ((0, 8),)),
        "offsets": draw_offsets(jax.random.fold_in(splits[4], 71), 0),
    }


def reference(bead_data, bead_cell, m2l_ops, offsets):
    moments = bead_data[:, 0, :].astype(jnp.float32)
    basis = bead_data[:, 1, :].astype(jnp.float32)
    total_cells = NZ * GX * GY
    multipole = jax.ops.segment_sum(moments, bead_cell, num_segments=total_cells).astype(jnp.bfloat16)
    grid = multipole.reshape(NZ, GX, GY, P_SIZE)
    padded = jnp.pad(grid, ((3, 3), (3, 3), (3, 3), (0, 0)))
    zero = jnp.zeros((), jnp.int32)

    def translate(total, item):
        matrix, shift = item
        starts = (shift[0] + 3, shift[1] + 3, shift[2] + 3, zero)
        window = lax.dynamic_slice(padded, starts, (NZ, GX, GY, P_SIZE)).reshape(total_cells, P_SIZE)
        return total + jnp.dot(window, matrix, preferred_element_type=jnp.float32), None

    local, _ = lax.scan(translate, jnp.zeros((total_cells, P_SIZE), jnp.float32), (m2l_ops, offsets))
    picked = local[bead_cell]
    return jnp.sum(picked * basis, axis=1) * (P_SIZE ** -0.5)
```

```python
import functools

import jax
import jax.numpy as jnp
import numpy as np
from jax import lax
from jax.experimental import pallas as pl
from jax.experimental.pallas import tpu as pltpu
from jax.sharding import Mesh, PartitionSpec as P

GX = 8
GY = 32
CZS = 4
RUN = 128
BF = jnp.bfloat16
F32 = jnp.float32

OWNERS = ("zh", "zl", "x", "y", "c")
SLABS = ("x", "zh", "zl")
GROUP = ("y", "c")
VMEM = pl.BlockSpec(memory_space=pltpu.VMEM)
SMEM = pl.BlockSpec(memory_space=pltpu.SMEM)


def one_hot(ids):
    lanes = lax.broadcasted_iota(jnp.int32, ids.shape, 1).astype(F32)
    return (ids.astype(F32) == lanes).astype(F32).astype(BF)


def sum_kernel(ids_ref, moments_ref, out_ref):
    cells = lax.dot_general(
        one_hot(ids_ref[...]),
        moments_ref[...],
        (((0,), (0,)), ((), ())),
        preferred_element_type=F32,
    ).astype(BF)
    for peer in range(out_ref.shape[0]):
        out_ref[peer] = cells


def m2l_kernel(offsets_ref, ops_ref, own_ref, low_ref, high_ref, out_ref, rows, shifted):
    shifted[:, :, 0:3] = jnp.zeros((6, 9, 3, GY, 128), BF)
    shifted[:, :, 11:13] = jnp.zeros((6, 9, 2, GY, 128), BF)
    rows[:, 0:8, :] = jnp.zeros((GX, 8, 128), F32)
    rows[:, 40:48, :] = jnp.zeros((GX, 8, 128), F32)
    for plane in range(9):
        ref, at = (low_ref, plane) if plane < 3 else (own_ref, plane - 3) if plane < 7 else (high_ref, plane - 7)
        rows[:, 8:40, :] = ref[at * 256 : (at + 1) * 256, :].astype(F32).reshape(GX, GY, 128)
        for dy in range(6):
            shifted[dy, plane, 3:11] = rows[:, 5 + dy : 37 + dy, :].astype(BF)
    ops = ops_ref[...].reshape(16 * 128, 128)
    for z in range(CZS):
        windows = []
        for k in range(16):
            dz, dx, dy = offsets_ref[k, 0], offsets_ref[k, 1], offsets_ref[k, 2]
            window = shifted[dy + 3, dz + (3 + z), pl.ds(dx + 3, GX)]
            windows.append(window.reshape(GX * GY, 128))
        total = jnp.dot(jnp.concatenate(windows, axis=1), ops, preferred_element_type=F32)
        out_ref[z * 256 : (z + 1) * 256, :] = total.astype(BF)


def field_kernel(ids_ref, basis_ref, parts_ref, out_ref):
    local = parts_ref[0].astype(F32)
    for peer in range(1, parts_ref.shape[0]):
        local = local + parts_ref[peer].astype(F32)
    high = local.astype(BF)
    low = (local - high.astype(F32)).astype(BF)
    pick = one_hot(ids_ref[...])
    picked = jnp.dot(pick, high, preferred_element_type=F32)
    picked = picked + jnp.dot(pick, low, preferred_element_type=F32)
    product = picked * basis_ref[...].astype(F32)
    out_ref[...] = jnp.sum(product.reshape(8, 128, 128), axis=2) * (128 ** -0.5)


def ops_moves():
    moves = []
    for z in range(16):
        for a in range(8):
            d = (a - z) % 8
            d = d - 8 if d > 4 else d
            moves.append((spot((z + d) % 16, (a + z) % 8), spot(z, a)))
    return moves


def spot(z, a):
    return (z // 8 * 8 + a) * 8 + z % 8


def slab_spot(s):
    return s % 4 * 16 + s // 4


def call(kernel, out_shape, in_specs, scratch=(), flops=0, size=0):
    return pl.pallas_call(
        kernel,
        out_shape=out_shape,
        in_specs=in_specs,
        out_specs=VMEM,
        scratch_shapes=list(scratch),
        compiler_params=pltpu.CompilerParams(vmem_limit_bytes=40 * 1024 * 1024),
        cost_estimate=pl.CostEstimate(flops=flops, bytes_accessed=size, transcendentals=0),
    )


def body(bead_data, bead_cell, m2l_ops, offsets):
    place = ("zh", "y", "c", "zl")
    ops = lax.ppermute(m2l_ops, place, ops_moves())
    shifts = lax.ppermute(offsets, place, ops_moves())

    inside = jnp.bitwise_and(bead_cell, RUN - 1).astype(BF).reshape(512, 1, 2, 1)
    inside = jnp.broadcast_to(inside, (512, 1, 2, 128))
    sent = jnp.concatenate([bead_data.reshape(512, 2, 2, 128), inside], axis=1)
    got = lax.all_to_all(sent.reshape(1536, 2, 128), OWNERS, split_axis=0, concat_axis=0, tiled=True)
    got = got.reshape(512, 3, 2, 128)
    moments = got[:, :2, 0].reshape(1024, 128)
    basis = got[:, :2, 1].reshape(1024, 128)
    ids = got[:, 2].reshape(1024, 128)

    cells = call(sum_kernel, jax.ShapeDtypeStruct((8, 128, 128), BF), [VMEM, VMEM])(ids, moments)
    slab = lax.all_to_all(cells, GROUP, split_axis=0, concat_axis=0, tiled=True).reshape(1024, 128)
    low = lax.ppermute(slab[256:], SLABS, [(slab_spot(i), slab_spot(i + 1)) for i in range(63)])
    high = lax.ppermute(slab[:512], SLABS, [(slab_spot(i + 1), slab_spot(i)) for i in range(63)])
    parts = call(
        m2l_kernel,
        jax.ShapeDtypeStruct((1024, 128), BF),
        [SMEM, VMEM, VMEM, VMEM, VMEM],
        [pltpu.VMEM((GX, 48, 128), F32), pltpu.VMEM((6, 9, 13, GY, 128), BF)],
    )(shifts, ops, slab, low, high)
    parts = lax.all_to_all(parts.reshape(8, 128, 128), GROUP, split_axis=0, concat_axis=0, tiled=True)
    field = call(field_kernel, jax.ShapeDtypeStruct((8, 128), F32), [VMEM, VMEM, VMEM])(ids, basis, parts)
    field = lax.all_to_all(field.reshape(512, 2), OWNERS, split_axis=0, concat_axis=0, tiled=True)
    return field.reshape(1024)


def solution(mesh):
    fine = Mesh(mesh.devices.reshape(4, 2, 4, 2, 8), ("x", "zh", "y", "c", "zl"))
    every = ("x", "zh", "y", "c", "zl")
    in_specs = (P(every, None, None), P(every), P("zl", None, None), P("zl", None))
    return jax.shard_map(body, mesh=fine, in_specs=in_specs, out_specs=P(every), check_vma=False)
```

```python
import functools

import jax
import jax.numpy as jnp
import numpy as np
from jax import lax
from jax.experimental import pallas as pl
from jax.experimental.pallas import tpu as pltpu
from jax.sharding import Mesh, PartitionSpec as P

GX = 8
GY = 32
CZS = 4
RUN = 128
BF = jnp.bfloat16
F32 = jnp.float32

COLUMN = ("zh", "zl")
LAYER = ("x", "y", "c")
SLABS = ("x", "zh", "zl")
GROUP = ("y", "c")
VMEM = pl.BlockSpec(memory_space=pltpu.VMEM)
SMEM = pl.BlockSpec(memory_space=pltpu.SMEM)


def iota(shape, dim):
    return lax.broadcasted_iota(jnp.int32, shape, dim)


def mask(where):
    return jnp.where(where, 1.0, 0.0)


def dot(a, b, dims=((1,), (0,)), precision=None):
    return lax.dot_general(a, b, (dims, ((), ())), precision=precision, preferred_element_type=F32)


def pack_kernel(offsets_ref, beads_ref, cells_ref, out_ref):
    for z in range(16):
        out_ref[z, 0:64] = beads_ref[64 * z : 64 * z + 64]
    inside = jnp.bitwise_and(cells_ref[...], RUN - 1).astype(F32)
    lane = iota((1, 128), 1)
    shifts = jnp.zeros((1, 128), F32)
    for k in range(16):
        for j in range(3):
            shifts = jnp.where(lane == 3 * k + j, offsets_ref[k, j].astype(F32), shifts)
    rows = []
    for z in range(16):
        rows += [inside[z // 2 : z // 2 + 1], shifts]
    out_ref[:, 64] = jnp.concatenate(rows, axis=0).astype(BF).reshape(16, 2, 128)


def regroup_kernel(place_ref, got_ref, out_ref, offsets_ref):
    core, half, shard = place_ref[0], place_ref[1], place_ref[2]
    for z in range(16):
        out_ref[:, 2 * z : 2 * z + 2] = got_ref[z, 0:64].reshape(32, 2, 2, 128)
    extra = got_ref[:, 64].reshape(32, 128)
    row, lane = iota((32, 128), 0), iota((32, 128), 1)
    take_row, take_lane = iota((64, 128), 0), iota((64, 128), 1)
    ids = jnp.zeros((64, 128), F32)
    for i in range(2):
        put = mask((row % 2 == 0) & (lane // 2 - 32 * core == row + i))
        take = mask((take_row % 2 == 0) & (take_lane == 64 * half + take_row + i))
        moved = dot(extra, put.astype(BF), ((0,), (0,)))
        ids = ids + dot(take.astype(BF), moved.astype(BF))
    out_ref[:, 32] = ids.astype(BF).reshape(32, 2, 128)
    out_ref[:, 33:40] = jnp.zeros((32, 7, 2, 128), BF)
    own = jnp.sum(mask(row == 2 * shard + 1) * extra.astype(F32), axis=0, keepdims=True)
    offsets_ref[...] = jnp.broadcast_to(own, (8, 128)).astype(jnp.int32)


def rows_of(got_ref, pair):
    at = 160 * pair
    return jnp.concatenate([got_ref[at : at + 64, :], got_ref[at + 80 : at + 144, :]], axis=0)


def sum_kernel(got_ref, cells_ref, ids_ref):
    cell, lane = iota((128, 128), 0), iota((128, 128), 1)
    even = lane % 2 == 0
    total = jnp.zeros((128, 128), F32)
    for pair in range(16):
        at = 160 * pair
        ids = got_ref[at + 64 : at + 80, :].astype(F32) + got_ref[at + 144 : at + 160, :].astype(F32)
        ids = ids[0:1]
        ids_ref[pair : pair + 1, :] = ids
        hot = mask((ids.astype(jnp.int32) == cell) & even).astype(BF)
        total = total + dot(hot, rows_of(got_ref, pair))
    cells = total.astype(BF)
    for peer in range(cells_ref.shape[0]):
        cells_ref[peer] = cells


def m2l_kernel(offsets_ref, ops_ref, own_ref, low_ref, high_ref, out_ref, rows, shifted):
    shifted[:, :, 0:3] = jnp.zeros((6, 9, 3, GY, 128), BF)
    shifted[:, :, 11:13] = jnp.zeros((6, 9, 2, GY, 128), BF)
    rows[:, 0:8, :] = jnp.zeros((GX, 8, 128), F32)
    rows[:, 40:48, :] = jnp.zeros((GX, 8, 128), F32)
    for plane in range(9):
        ref, at = (low_ref, plane) if plane < 3 else (own_ref, plane - 3) if plane < 7 else (high_ref, plane - 7)
        rows[:, 8:40, :] = ref[at * 256 : (at + 1) * 256, :].astype(F32).reshape(GX, GY, 128)
        for dy in range(6):
            shifted[dy, plane, 3:11] = rows[:, 5 + dy : 37 + dy, :].astype(BF)
    ops = ops_ref[...].reshape(16 * 128, 128)
    for z in range(CZS):
        windows = []
        for k in range(16):
            dz, dx, dy = offsets_ref[0, 3 * k], offsets_ref[0, 3 * k + 1], offsets_ref[0, 3 * k + 2]
            window = shifted[dy + 3, dz + (3 + z), pl.ds(dx + 3, GX)]
            windows.append(window.reshape(GX * GY, 128))
        total = jnp.dot(jnp.concatenate(windows, axis=1), ops, preferred_element_type=F32)
        out_ref[z * 256 : (z + 1) * 256, :] = total.astype(BF)


def field_kernel(ids_ref, got_ref, parts_ref, out_ref):
    local = parts_ref[0].astype(F32)
    for peer in range(1, parts_ref.shape[0]):
        local = local + parts_ref[peer].astype(F32)
    high = local.astype(BF)
    low = (local - high.astype(F32)).astype(BF)
    split = jnp.concatenate([high, low], axis=0)
    cell, lane = iota((128, 128), 0), iota((128, 128), 1)
    odd = lane % 2 == 1
    for pair in range(16):
        every = dot(split, rows_of(got_ref, pair), ((1,), (1,)))
        every = every[0:128] + every[128:256]
        hot = (ids_ref[pair : pair + 1, :].astype(jnp.int32) == cell) & odd
        field = jnp.sum(jnp.where(hot, every, 0.0), axis=0, keepdims=True) * (128 ** -0.5)
        out_ref[2 * pair : 2 * pair + 1, :] = field
        out_ref[2 * pair + 1 : 2 * pair + 2, :] = field


def return_kernel(place_ref, got_ref, out_ref):
    core, half = place_ref[0], place_ref[1]
    exact = lax.Precision.HIGHEST
    z, lane = iota((16, 128), 0), iota((16, 128), 1)
    owner, column = iota((32, 128), 0), iota((32, 128), 1)
    total = jnp.zeros((16, 128), F32)
    for i in range(2):
        take = mask(lane == 64 * core + 4 * z + 2 * i + 1)
        put = mask(column == 64 * half + 2 * owner + i)
        total = total + dot(dot(take, got_ref[...], ((1,), (1,)), exact), put, precision=exact)
    out_ref[...] = total


def join_kernel(got_ref, out_ref):
    for k in range(8):
        out_ref[k : k + 1, :] = got_ref[2 * k : 2 * k + 1, :] + got_ref[2 * k + 1 : 2 * k + 2, :]


def ops_moves():
    moves = []
    for z in range(16):
        for a in range(8):
            d = (a - z) % 8
            d = d - 8 if d > 4 else d
            moves.append((spot((z + d) % 16, (a + z) % 8), spot(z, a)))
    return moves


def spot(z, a):
    return (z // 8 * 8 + a) * 8 + z % 8


def slab_spot(s):
    return s % 4 * 16 + s // 4


def call(kernel, out_shape, in_specs, scratch=()):
    many = isinstance(out_shape, list)
    return pl.pallas_call(
        kernel,
        out_shape=out_shape,
        in_specs=in_specs,
        out_specs=[VMEM] * len(out_shape) if many else VMEM,
        scratch_shapes=list(scratch),
        compiler_params=pltpu.CompilerParams(vmem_limit_bytes=40 * 1024 * 1024),
    )


def shape(*size, kind=BF):
    return jax.ShapeDtypeStruct(size, kind)


def exchange(array, axes):
    return lax.all_to_all(array, axes, split_axis=0, concat_axis=0, tiled=True)


def body(bead_data, bead_cell, m2l_ops, offsets):
    core = lax.axis_index("c")
    place = jnp.stack([core, lax.axis_index("zl") % 2, lax.axis_index("y") * 2 + core])

    sent = call(pack_kernel, shape(16, 65, 2, 128), [SMEM, VMEM, VMEM])(
        offsets, bead_data, bead_cell.reshape(8, 128)
    )
    got = exchange(sent.reshape(1040, 2, 128), COLUMN)
    m2l_ops, got = lax.optimization_barrier((m2l_ops, got))
    ops = lax.ppermute(m2l_ops, ("zh", "y", "c", "zl"), ops_moves())
    sent, shifts = call(
        regroup_kernel, [shape(32, 40, 2, 128), shape(8, 128, kind=jnp.int32)], [SMEM, VMEM]
    )(place, got.reshape(16, 65, 2, 128))
    rows = exchange(sent.reshape(1280, 2, 128), LAYER).reshape(2560, 128)

    cells, ids = call(sum_kernel, [shape(8, 128, 128), shape(16, 128, kind=F32)], [VMEM])(rows)
    slab = exchange(cells, GROUP).reshape(1024, 128)
    low = lax.ppermute(slab[256:], SLABS, [(slab_spot(i), slab_spot(i + 1)) for i in range(63)])
    high = lax.ppermute(slab[:512], SLABS, [(slab_spot(i + 1), slab_spot(i)) for i in range(63)])
    parts = call(
        m2l_kernel,
        shape(1024, 128),
        [SMEM, VMEM, VMEM, VMEM, VMEM],
        [pltpu.VMEM((GX, 48, 128), F32), pltpu.VMEM((6, 9, 13, GY, 128), BF)],
    )(shifts, ops, slab, low, high)
    parts = exchange(parts.reshape(8, 128, 128), GROUP)
    field = call(field_kernel, shape(32, 128, kind=F32), [VMEM, VMEM, VMEM])(ids, rows, parts)
    field = exchange(field, LAYER)
    field = call(return_kernel, shape(16, 128, kind=F32), [SMEM, VMEM])(place, field)
    field = exchange(field, COLUMN)
    return call(join_kernel, shape(8, 128, kind=F32), [VMEM])(field).reshape(1024)


def solution(mesh):
    fine = Mesh(mesh.devices.reshape(4, 2, 4, 2, 8), ("x", "zh", "y", "c", "zl"))
    every = ("x", "zh", "y", "c", "zl")
    in_specs = (P(every, None, None), P(every), P("zl", None, None), P("zl", None))
    return jax.shard_map(body, mesh=fine, in_specs=in_specs, out_specs=P(every), check_vma=False)
```

```python
import functools

import jax
import jax.numpy as jnp
import numpy as np
from jax import lax
from jax.experimental import pallas as pl
from jax.experimental.pallas import tpu as pltpu
from jax.sharding import Mesh, PartitionSpec as P

GX = 8
GY = 32
CZS = 4
RUN = 128
BF = jnp.bfloat16
F32 = jnp.float32

COLUMN = ("zh", "zl")
LAYER = ("x", "y", "c")
SLABS = ("x", "zh", "zl")
GROUP = ("y", "c")
VMEM = pl.BlockSpec(memory_space=pltpu.VMEM)
SMEM = pl.BlockSpec(memory_space=pltpu.SMEM)


def iota(shape, dim):
    return lax.broadcasted_iota(jnp.int32, shape, dim)


def mask(where):
    return jnp.where(where, 1.0, 0.0)


def dot(a, b, dims=((1,), (0,)), precision=None):
    return lax.dot_general(a, b, (dims, ((), ())), precision=precision, preferred_element_type=F32)


def pack_kernel(offsets_ref, rows_ref, cells_ref, moments_ref):
    to, at = iota((64, 128), 0), iota((64, 128), 1)
    part = mask(at == 2 * to).astype(BF)
    for z in range(16):
        moments_ref[z, 0:32] = dot(part, rows_ref[128 * z : 128 * z + 128, :]).astype(BF).reshape(32, 2, 128)
    inside = jnp.bitwise_and(cells_ref[...], RUN - 1).astype(F32)
    lane = iota((1, 128), 1)
    shifts = jnp.zeros((1, 128), F32)
    for k in range(16):
        for j in range(3):
            shifts = jnp.where(lane == 3 * k + j, offsets_ref[j, k].astype(F32), shifts)
    rows = []
    for z in range(16):
        rows += [inside[z // 2 : z // 2 + 1], shifts]
    moments_ref[:, 32] = jnp.concatenate(rows, axis=0).astype(BF).reshape(16, 2, 128)


def regroup_kernel(place_ref, got_ref, out_ref, offsets_ref):
    quarter, half, shard = place_ref[0], place_ref[1], place_ref[2]
    for z in range(16):
        out_ref[:, z] = got_ref[z, 0:32]
    extra = got_ref[:, 32].reshape(32, 128)
    row, lane = iota((32, 128), 0), iota((32, 128), 1)
    take_row, take_lane = iota((64, 128), 0), iota((64, 128), 1)
    ids = jnp.zeros((64, 128), F32)
    for i in range(2):
        put = mask((row % 2 == 0) & (lane - 32 * quarter == row + i))
        take = mask((take_row % 2 == 0) & (take_lane == 64 * half + take_row + i))
        moved = dot(extra, put.astype(BF), ((0,), (0,)))
        ids = ids + dot(take.astype(BF), moved.astype(BF))
    out_ref[:, 16] = ids.astype(BF).reshape(32, 2, 128)
    out_ref[:, 17:24] = jnp.zeros((32, 7, 2, 128), BF)
    own = jnp.sum(mask(row == 2 * shard + 1) * extra.astype(F32), axis=0, keepdims=True)
    offsets_ref[...] = jnp.broadcast_to(own, (8, 128)).astype(jnp.int32)


def sum_kernel(got_ref, cells_ref, ids_ref):
    cell = iota((128, 128), 0)
    total = jnp.zeros((128, 128), F32)
    for four in range(8):
        blocks = [got_ref[4 * four + j] for j in range(4)]
        ids = sum(block[32:48].astype(F32) for block in blocks)[0:1]
        ids_ref[four : four + 1, :] = ids
        hot = mask(ids.astype(jnp.int32) == cell).astype(BF)
        total = total + dot(hot, jnp.concatenate([block[0:32] for block in blocks], axis=0))
    cells = total.astype(BF)
    for peer in range(cells_ref.shape[0]):
        cells_ref[peer] = cells


def m2l_kernel(offsets_ref, ops_ref, own_ref, low_ref, high_ref, out_ref, rows, shifted):
    shifted[:, :, 0:3] = jnp.zeros((6, 9, 3, GY, 128), BF)
    shifted[:, :, 11:13] = jnp.zeros((6, 9, 2, GY, 128), BF)
    rows[:, 0:8, :] = jnp.zeros((GX, 8, 128), F32)
    rows[:, 40:48, :] = jnp.zeros((GX, 8, 128), F32)
    for plane in range(9):
        ref, at = (low_ref, plane) if plane < 3 else (own_ref, plane - 3) if plane < 7 else (high_ref, plane - 7)
        rows[:, 8:40, :] = ref[at * 256 : (at + 1) * 256, :].astype(F32).reshape(GX, GY, 128)
        for dy in range(6):
            shifted[dy, plane, 3:11] = rows[:, 5 + dy : 37 + dy, :].astype(BF)
    ops = ops_ref[...].reshape(16 * 128, 128)
    for z in range(CZS):
        windows = []
        for k in range(16):
            dz, dx, dy = offsets_ref[0, 3 * k], offsets_ref[0, 3 * k + 1], offsets_ref[0, 3 * k + 2]
            window = shifted[dy + 3, dz + (3 + z), pl.ds(dx + 3, GX)]
            windows.append(window.reshape(GX * GY, 128))
        total = jnp.dot(jnp.concatenate(windows, axis=1), ops, preferred_element_type=F32)
        out_ref[z * 256 : (z + 1) * 256, :] = total.astype(BF)


def pick_kernel(ids_ref, parts_ref, out_ref):
    local = parts_ref[0].astype(F32)
    for peer in range(1, parts_ref.shape[0]):
        local = local + parts_ref[peer].astype(F32)
    local = local.astype(BF)
    cell = iota((128, 128), 0)
    for four in range(8):
        hot = mask(ids_ref[four : four + 1, :].astype(jnp.int32) == cell).astype(BF)
        out_ref[128 * four : 128 * four + 128, :] = dot(hot, local, ((0,), (0,))).astype(BF)


def return_kernel(got_ref, out_ref):
    for z in range(16):
        out_ref[z] = got_ref[:, z]


def field_kernel(rows_ref, picked_ref, out_ref):
    to, at = iota((128, 256), 0), iota((128, 256), 1)
    part = mask(at == 2 * to + 1).astype(BF)
    ones = jnp.ones((8, 128), BF)
    for k in range(8):
        basis = dot(part, rows_ref[256 * k : 256 * k + 256, :])
        product = basis * picked_ref[128 * k : 128 * k + 128, :].astype(F32)
        high = product.astype(BF)
        low = (product - high.astype(F32)).astype(BF)
        field = dot(ones, high, ((1,), (1,))) + dot(ones, low, ((1,), (1,)))
        out_ref[k : k + 1, :] = field[0:1] * (128 ** -0.5)


def ops_moves():
    moves = []
    for z in range(16):
        for a in range(8):
            d = (a - z) % 8
            d = d - 8 if d > 4 else d
            moves.append((spot((z + d) % 16, (a + z) % 8), spot(z, a)))
    return moves


def spot(z, a):
    return (z // 8 * 8 + a) * 8 + z % 8


def slab_spot(s):
    return s % 4 * 16 + s // 4


def call(kernel, out_shape, in_specs, scratch=()):
    many = isinstance(out_shape, list)
    return pl.pallas_call(
        kernel,
        out_shape=out_shape,
        in_specs=in_specs,
        out_specs=[VMEM] * len(out_shape) if many else VMEM,
        scratch_shapes=list(scratch),
        compiler_params=pltpu.CompilerParams(vmem_limit_bytes=40 * 1024 * 1024),
    )


def shape(*size, kind=BF):
    return jax.ShapeDtypeStruct(size, kind)


def exchange(array, axes):
    return lax.all_to_all(array, axes, split_axis=0, concat_axis=0, tiled=True)


def body(bead_data, bead_cell, m2l_ops, offsets):
    shard = lax.axis_index("y") * 2 + lax.axis_index("c")
    place = jnp.stack([shard % 4, lax.axis_index("zl") % 2, shard])

    rows = bead_data.reshape(2048, 128)
    moments = call(pack_kernel, shape(16, 33, 2, 128), [SMEM, VMEM, VMEM])(
        offsets.T, rows, bead_cell.reshape(8, 128)
    )
    moments = exchange(moments.reshape(528, 2, 128), COLUMN)
    m2l_ops, moments = lax.optimization_barrier((m2l_ops, moments))
    moments, shifts = call(
        regroup_kernel, [shape(32, 24, 2, 128), shape(8, 128, kind=jnp.int32)], [SMEM, VMEM]
    )(place, moments.reshape(16, 33, 2, 128))
    moments = exchange(moments.reshape(768, 2, 128), LAYER).reshape(32, 48, 128)
    ops = lax.ppermute(m2l_ops, ("zh", "y", "c", "zl"), ops_moves())
    cells, ids = call(sum_kernel, [shape(8, 128, 128), shape(8, 128, kind=F32)], [VMEM])(moments)
    slab = exchange(cells, GROUP).reshape(1024, 128)
    low = lax.ppermute(slab[256:], SLABS, [(slab_spot(i), slab_spot(i + 1)) for i in range(63)])
    high = lax.ppermute(slab[:512], SLABS, [(slab_spot(i + 1), slab_spot(i)) for i in range(63)])
    parts = call(
        m2l_kernel,
        shape(1024, 128),
        [SMEM, VMEM, VMEM, VMEM, VMEM],
        [pltpu.VMEM((GX, 48, 128), F32), pltpu.VMEM((6, 9, 13, GY, 128), BF)],
    )(shifts, ops, slab, low, high)
    parts = exchange(parts.reshape(8, 128, 128), GROUP)
    picked = call(pick_kernel, shape(1024, 128), [VMEM, VMEM])(ids, parts)
    picked = exchange(picked.reshape(512, 2, 128), LAYER)
    picked = call(return_kernel, shape(16, 32, 2, 128), [VMEM])(picked.reshape(32, 16, 2, 128))
    picked = exchange(picked.reshape(512, 2, 128), COLUMN).reshape(1024, 128)
    return call(field_kernel, shape(8, 128, kind=F32), [VMEM, VMEM])(rows, picked).reshape(1024)


def solution(mesh):
    fine = Mesh(mesh.devices.reshape(4, 2, 4, 2, 8), ("x", "zh", "y", "c", "zl"))
    every = ("x", "zh", "y", "c", "zl")
    in_specs = (P(every, None, None), P(every), P("zl", None, None), P("zl", None))
    return jax.shard_map(body, mesh=fine, in_specs=in_specs, out_specs=P(every), check_vma=False)
```

```python
import functools

import jax
import jax.numpy as jnp
import numpy as np
from jax import lax
from jax.experimental import pallas as pl
from jax.experimental.pallas import tpu as pltpu
from jax.sharding import Mesh, PartitionSpec as P

GX = 8
GY = 32
CZS = 4
RUN = 128
BF = jnp.bfloat16
F32 = jnp.float32

COLUMN = ("zh", "zl")
LAYER = ("x", "y", "c")
SLABS = ("x", "zh", "zl")
GROUP = ("y", "c")
VMEM = pl.BlockSpec(memory_space=pltpu.VMEM)
SMEM = pl.BlockSpec(memory_space=pltpu.SMEM)


def iota(shape, dim):
    return lax.broadcasted_iota(jnp.int32, shape, dim)


def mask(where):
    return jnp.where(where, 1.0, 0.0)


def dot(a, b, dims=((1,), (0,)), precision=None):
    return lax.dot_general(a, b, (dims, ((), ())), precision=precision, preferred_element_type=F32)


def pack_kernel(offsets_ref, rows_ref, cells_ref, moments_ref):
    to, at = iota((64, 128), 0), iota((64, 128), 1)
    part = mask(at == 2 * to).astype(BF)
    for z in range(16):
        moments_ref[z, 0:32] = dot(part, rows_ref[128 * z : 128 * z + 128, :]).astype(BF).reshape(32, 2, 128)
    inside = jnp.bitwise_and(cells_ref[...], RUN - 1).astype(F32)
    lane = iota((1, 128), 1)
    shifts = jnp.zeros((1, 128), F32)
    for k in range(16):
        for j in range(3):
            shifts = jnp.where(lane == 3 * k + j, offsets_ref[j, k].astype(F32), shifts)
    rows = []
    for z in range(16):
        rows += [inside[z // 2 : z // 2 + 1], shifts]
    moments_ref[:, 32] = jnp.concatenate(rows, axis=0).astype(BF).reshape(16, 2, 128)


def regroup_kernel(place_ref, got_ref, out_ref, offsets_ref):
    quarter, half, shard = place_ref[0], place_ref[1], place_ref[2]
    for z in range(16):
        out_ref[:, z] = got_ref[z, 0:32]
    extra = got_ref[:, 32].reshape(32, 128)
    row, lane = iota((32, 128), 0), iota((32, 128), 1)
    take_row, take_lane = iota((64, 128), 0), iota((64, 128), 1)
    ids = jnp.zeros((64, 128), F32)
    for i in range(2):
        put = mask((row % 2 == 0) & (lane - 32 * quarter == row + i))
        take = mask((take_row % 2 == 0) & (take_lane == 64 * half + take_row + i))
        moved = dot(extra, put.astype(BF), ((0,), (0,)))
        ids = ids + dot(take.astype(BF), moved.astype(BF))
    out_ref[:, 16] = ids.astype(BF).reshape(32, 2, 128)
    out_ref[:, 17:24] = jnp.zeros((32, 7, 2, 128), BF)
    own = jnp.sum(mask(row == 2 * shard + 1) * extra.astype(F32), axis=0, keepdims=True)
    offsets_ref[...] = jnp.broadcast_to(own, (8, 128)).astype(jnp.int32)


def sum_kernel(got_ref, cells_ref, ids_ref):
    cell = iota((128, 128), 0)
    total = jnp.zeros((128, 128), F32)
    for four in range(8):
        blocks = [got_ref[4 * four + j] for j in range(4)]
        ids = sum(block[32:48].astype(F32) for block in blocks)[0:1]
        ids_ref[four : four + 1, :] = ids
        hot = mask(ids.astype(jnp.int32) == cell).astype(BF)
        total = total + dot(hot, jnp.concatenate([block[0:32] for block in blocks], axis=0))
    cells = total.astype(BF)
    for peer in range(cells_ref.shape[0]):
        cells_ref[peer] = cells


def m2l_kernel(offsets_ref, ops_ref, own_ref, low_ref, high_ref, out_ref, rows, shifted):
    shifted[:, :, 0:3] = jnp.zeros((6, 9, 3, GY, 128), BF)
    shifted[:, :, 11:13] = jnp.zeros((6, 9, 2, GY, 128), BF)
    rows[:, 0:8, :] = jnp.zeros((GX, 8, 128), F32)
    rows[:, 40:48, :] = jnp.zeros((GX, 8, 128), F32)
    for plane in range(9):
        ref, at = (low_ref, plane) if plane < 3 else (own_ref, plane - 3) if plane < 7 else (high_ref, plane - 7)
        rows[:, 8:40, :] = ref[at * 256 : (at + 1) * 256, :].astype(F32).reshape(GX, GY, 128)
        for dy in range(6):
            shifted[dy, plane, 3:11] = rows[:, 5 + dy : 37 + dy, :].astype(BF)
    ops = ops_ref[...].reshape(16 * 128, 128)
    for z in range(CZS):
        windows = []
        for k in range(16):
            dz, dx, dy = offsets_ref[0, 3 * k], offsets_ref[0, 3 * k + 1], offsets_ref[0, 3 * k + 2]
            window = shifted[dy + 3, dz + (3 + z), pl.ds(dx + 3, GX)]
            windows.append(window.reshape(GX * GY, 128))
        total = jnp.dot(jnp.concatenate(windows, axis=1), ops, preferred_element_type=F32)
        out_ref[z * 256 : (z + 1) * 256, :] = total.astype(BF)


def pick_kernel(ids_ref, parts_ref, out_ref):
    local = parts_ref[0].astype(F32)
    for peer in range(1, parts_ref.shape[0]):
        local = local + parts_ref[peer].astype(F32)
    local = local.astype(BF)
    cell = iota((128, 128), 0)
    for four in range(8):
        hot = mask(ids_ref[four : four + 1, :].astype(jnp.int32) == cell).astype(BF)
        out_ref[128 * four : 128 * four + 128, :] = dot(hot, local, ((0,), (0,))).astype(BF)


def return_kernel(got_ref, out_ref):
    for z in range(16):
        out_ref[z] = got_ref[:, z]


def field_kernel(rows_ref, picked_ref, out_ref):
    to, at = iota((128, 256), 0), iota((128, 256), 1)
    part = mask(at == 2 * to + 1).astype(BF)
    ones = jnp.ones((8, 128), BF)
    for k in range(8):
        basis = dot(part, rows_ref[256 * k : 256 * k + 256, :])
        product = basis * picked_ref[128 * k : 128 * k + 128, :].astype(F32)
        high = product.astype(BF)
        low = (product - high.astype(F32)).astype(BF)
        field = dot(ones, high, ((1,), (1,))) + dot(ones, low, ((1,), (1,)))
        out_ref[k : k + 1, :] = field[0:1] * (128 ** -0.5)


REACH = (0, 4, 1, -1, 2, -2, 3, -3)


def ops_moves():
    return [(spot((z + REACH[a]) % 16, a), spot(z, a)) for z in range(16) for a in range(8)]


def spot(z, a):
    return (z // 8 * 8 + a) * 8 + z % 8


def slab_spot(s):
    return s % 4 * 16 + s // 4


def call(kernel, out_shape, in_specs, scratch=()):
    many = isinstance(out_shape, list)
    return pl.pallas_call(
        kernel,
        out_shape=out_shape,
        in_specs=in_specs,
        out_specs=[VMEM] * len(out_shape) if many else VMEM,
        scratch_shapes=list(scratch),
        compiler_params=pltpu.CompilerParams(vmem_limit_bytes=40 * 1024 * 1024),
    )


def shape(*size, kind=BF):
    return jax.ShapeDtypeStruct(size, kind)


def exchange(array, axes):
    return lax.all_to_all(array, axes, split_axis=0, concat_axis=0, tiled=True)


def body(bead_data, bead_cell, m2l_ops, offsets):
    peer = lax.axis_index("y") * 2 + lax.axis_index("c")
    layer = lax.axis_index("zl")
    shard = (layer + 8 + jnp.array(REACH, jnp.int32)[peer]) % 8
    place = jnp.stack([peer % 4, layer % 2, shard])

    rows = bead_data.reshape(2048, 128)
    moments = call(pack_kernel, shape(16, 33, 2, 128), [SMEM, VMEM, VMEM])(
        offsets.T, rows, bead_cell.reshape(8, 128)
    )
    moments = exchange(moments.reshape(528, 2, 128), COLUMN)
    m2l_ops, moments = lax.optimization_barrier((m2l_ops, moments))
    moments, shifts = call(
        regroup_kernel, [shape(32, 24, 2, 128), shape(8, 128, kind=jnp.int32)], [SMEM, VMEM]
    )(place, moments.reshape(16, 33, 2, 128))
    moments = exchange(moments.reshape(768, 2, 128), LAYER).reshape(32, 48, 128)
    ops = lax.ppermute(m2l_ops, ("zh", "y", "c", "zl"), ops_moves())
    cells, ids = call(sum_kernel, [shape(8, 128, 128), shape(8, 128, kind=F32)], [VMEM])(moments)
    slab = exchange(cells, GROUP).reshape(1024, 128)
    low = lax.ppermute(slab[256:], SLABS, [(slab_spot(i), slab_spot(i + 1)) for i in range(63)])
    high = lax.ppermute(slab[:512], SLABS, [(slab_spot(i + 1), slab_spot(i)) for i in range(63)])
    parts = call(
        m2l_kernel,
        shape(1024, 128),
        [SMEM, VMEM, VMEM, VMEM, VMEM],
        [pltpu.VMEM((GX, 48, 128), F32), pltpu.VMEM((6, 9, 13, GY, 128), BF)],
    )(shifts, ops, slab, low, high)
    parts = exchange(parts.reshape(8, 128, 128), GROUP)
    picked = call(pick_kernel, shape(1024, 128), [VMEM, VMEM])(ids, parts)
    picked = exchange(picked.reshape(512, 2, 128), LAYER)
    picked = call(return_kernel, shape(16, 32, 2, 128), [VMEM])(picked.reshape(32, 16, 2, 128))
    picked = exchange(picked.reshape(512, 2, 128), COLUMN).reshape(1024, 128)
    return call(field_kernel, shape(8, 128, kind=F32), [VMEM, VMEM])(rows, picked).reshape(1024)


def solution(mesh):
    fine = Mesh(mesh.devices.reshape(4, 2, 4, 2, 8), ("x", "zh", "y", "c", "zl"))
    every = ("x", "zh", "y", "c", "zl")
    in_specs = (P(every, None, None), P(every), P("zl", None, None), P("zl", None))
    return jax.shard_map(body, mesh=fine, in_specs=in_specs, out_specs=P(every), check_vma=False)
```

```python
import functools

import jax
import jax.numpy as jnp
import numpy as np
from jax import lax
from jax.experimental import pallas as pl
from jax.experimental.pallas import tpu as pltpu
from jax.sharding import Mesh, PartitionSpec as P

GX = 8
GY = 32
CZS = 4
RUN = 128
BF = jnp.bfloat16
F32 = jnp.float32

COLUMN = ("zh", "zl")
LAYER = ("x", "y", "c")
SLABS = ("x", "zh", "zl")
GROUP = ("y", "c")
VMEM = pl.BlockSpec(memory_space=pltpu.VMEM)
SMEM = pl.BlockSpec(memory_space=pltpu.SMEM)


def iota(shape, dim):
    return lax.broadcasted_iota(jnp.int32, shape, dim)


def mask(where):
    return jnp.where(where, 1.0, 0.0)


def dot(a, b, dims=((1,), (0,)), precision=None):
    return lax.dot_general(a, b, (dims, ((), ())), precision=precision, preferred_element_type=F32)


def pack_kernel(offsets_ref, rows_ref, cells_ref, moments_ref):
    to, at = iota((64, 128), 0), iota((64, 128), 1)
    part = mask(at == 2 * to).astype(BF)
    for z in range(16):
        moments_ref[z, 0:32] = dot(part, rows_ref[128 * z : 128 * z + 128, :]).astype(BF).reshape(32, 2, 128)
    inside = jnp.bitwise_and(cells_ref[...], RUN - 1).astype(F32)
    lane = iota((1, 128), 1)
    shifts = jnp.zeros((1, 128), F32)
    for k in range(16):
        for j in range(3):
            shifts = jnp.where(lane == 3 * k + j, offsets_ref[j, k].astype(F32), shifts)
    rows = []
    for z in range(16):
        rows += [inside[z // 2 : z // 2 + 1], shifts]
    moments_ref[:, 32] = jnp.concatenate(rows, axis=0).astype(BF).reshape(16, 2, 128)


def regroup_kernel(got_ref, out_ref, offsets_ref):
    peer, layer = lax.axis_index("y") * 2 + lax.axis_index("c"), lax.axis_index("zl")
    quarter, half = lax.rem(peer, 4), lax.rem(layer, 2)
    reach = jnp.int32(0)
    for a in range(8):
        reach = jnp.where(peer == a, REACH[a] % 8, reach)
    shard = lax.rem(layer + reach, 8)
    for z in range(16):
        out_ref[:, z] = got_ref[z, 0:32]
    extra = got_ref[:, 32].reshape(32, 128)
    row, lane = iota((32, 128), 0), iota((32, 128), 1)
    take_row, take_lane = iota((64, 128), 0), iota((64, 128), 1)
    ids = jnp.zeros((64, 128), F32)
    for i in range(2):
        put = mask((row % 2 == 0) & (lane - 32 * quarter == row + i))
        take = mask((take_row % 2 == 0) & (take_lane == 64 * half + take_row + i))
        taken = dot(take.astype(BF), extra, ((1,), (1,)))
        ids = ids + dot(taken.astype(BF), put.astype(BF))
    out_ref[:, 16] = ids.astype(BF).reshape(32, 2, 128)
    out_ref[:, 17:24] = jnp.zeros((32, 7, 2, 128), BF)
    own = jnp.sum(mask(row == 2 * shard + 1) * extra.astype(F32), axis=0, keepdims=True)
    offsets_ref[...] = jnp.broadcast_to(own, (8, 128)).astype(jnp.int32)


def sum_kernel(got_ref, cells_ref, ids_ref):
    cell = iota((128, 128), 0)
    total = jnp.zeros((128, 128), F32)
    for four in range(8):
        blocks = [got_ref[4 * four + j] for j in range(4)]
        ids = sum(block[32:48].astype(F32) for block in blocks)[0:1]
        ids_ref[four : four + 1, :] = ids
        hot = mask(ids.astype(jnp.int32) == cell).astype(BF)
        total = total + dot(hot, jnp.concatenate([block[0:32] for block in blocks], axis=0))
    cells = total.astype(BF)
    for peer in range(cells_ref.shape[0]):
        cells_ref[peer] = cells


def m2l_kernel(offsets_ref, ops_ref, own_ref, low_ref, high_ref, out_ref, rows, shifted):
    shifted[:, :, 0:3] = jnp.zeros((6, 9, 3, GY, 128), BF)
    shifted[:, :, 11:13] = jnp.zeros((6, 9, 2, GY, 128), BF)
    rows[:, 0:8, :] = jnp.zeros((GX, 8, 128), F32)
    rows[:, 40:48, :] = jnp.zeros((GX, 8, 128), F32)
    for plane in range(9):
        ref, at = (low_ref, plane) if plane < 3 else (own_ref, plane - 3) if plane < 7 else (high_ref, plane - 7)
        rows[:, 8:40, :] = ref[at * 256 : (at + 1) * 256, :].astype(F32).reshape(GX, GY, 128)
        for dy in range(6):
            shifted[dy, plane, 3:11] = rows[:, 5 + dy : 37 + dy, :].astype(BF)
    ops = ops_ref[...].reshape(16 * 128, 128)
    for z in range(CZS):
        windows = []
        for k in range(16):
            dz, dx, dy = offsets_ref[0, 3 * k], offsets_ref[0, 3 * k + 1], offsets_ref[0, 3 * k + 2]
            window = shifted[dy + 3, dz + (3 + z), pl.ds(dx + 3, GX)]
            windows.append(window.reshape(GX * GY, 128))
        total = jnp.dot(jnp.concatenate(windows, axis=1), ops, preferred_element_type=F32)
        out_ref[z * 256 : (z + 1) * 256, :] = total.astype(BF)


def pick_kernel(ids_ref, parts_ref, out_ref):
    local = parts_ref[0].astype(F32)
    for peer in range(1, parts_ref.shape[0]):
        local = local + parts_ref[peer].astype(F32)
    local = local.astype(BF)
    cell = iota((128, 128), 0)
    for four in range(8):
        hot = mask(ids_ref[four : four + 1, :].astype(jnp.int32) == cell).astype(BF)
        out_ref[128 * four : 128 * four + 128, :] = dot(hot, local, ((0,), (0,))).astype(BF)


def field_kernel(rows_ref, picked_ref, out_ref):
    to, at = iota((128, 256), 0), iota((128, 256), 1)
    part = mask(at == 2 * to + 1).astype(BF)
    for k in range(8):
        basis = dot(part, rows_ref[256 * k : 256 * k + 256, :])
        picked = [picked_ref[:, 2 * k + j].reshape(64, 128) for j in range(2)]
        product = basis * jnp.concatenate(picked, axis=0).astype(F32)
        out_ref[k : k + 1, :] = jnp.sum(product, axis=1)[None] * (128 ** -0.5)


REACH = (0, 4, 1, -1, 2, -2, 3, -3)


def ops_moves():
    return [(spot((z + REACH[a]) % 16, a), spot(z, a)) for z in range(16) for a in range(8)]


def spot(z, a):
    return (z // 8 * 8 + a) * 8 + z % 8


def slab_spot(s):
    return s % 4 * 16 + s // 4


def call(kernel, out_shape, in_specs, scratch=()):
    many = isinstance(out_shape, list)
    return pl.pallas_call(
        kernel,
        out_shape=out_shape,
        in_specs=in_specs,
        out_specs=[VMEM] * len(out_shape) if many else VMEM,
        scratch_shapes=list(scratch),
        compiler_params=pltpu.CompilerParams(vmem_limit_bytes=40 * 1024 * 1024),
    )


def shape(*size, kind=BF):
    return jax.ShapeDtypeStruct(size, kind)


def exchange(array, axes):
    return lax.all_to_all(array, axes, split_axis=0, concat_axis=0, tiled=True)


def body(bead_data, bead_cell, m2l_ops, offsets):
    rows = bead_data.reshape(2048, 128)
    moments = call(pack_kernel, shape(16, 33, 2, 128), [SMEM, VMEM, VMEM])(
        offsets.T, rows, bead_cell.reshape(8, 128)
    )
    moments = exchange(moments.reshape(528, 2, 128), COLUMN)
    m2l_ops, moments = lax.optimization_barrier((m2l_ops, moments))
    moments, shifts = call(
        regroup_kernel, [shape(32, 24, 2, 128), shape(8, 128, kind=jnp.int32)], [VMEM]
    )(moments.reshape(16, 33, 2, 128))
    moments = exchange(moments.reshape(768, 2, 128), LAYER).reshape(32, 48, 128)
    ops = lax.ppermute(m2l_ops, ("zh", "y", "c", "zl"), ops_moves())
    cells, ids = call(sum_kernel, [shape(8, 128, 128), shape(8, 128, kind=F32)], [VMEM])(moments)
    slab = exchange(cells, GROUP).reshape(1024, 128)
    low = lax.ppermute(slab[256:], SLABS, [(slab_spot(i), slab_spot(i + 1)) for i in range(63)])
    high = lax.ppermute(slab[:512], SLABS, [(slab_spot(i + 1), slab_spot(i)) for i in range(63)])
    parts = call(
        m2l_kernel,
        shape(1024, 128),
        [SMEM, VMEM, VMEM, VMEM, VMEM],
        [pltpu.VMEM((GX, 48, 128), F32), pltpu.VMEM((6, 9, 13, GY, 128), BF)],
    )(shifts, ops, slab, low, high)
    parts = exchange(parts.reshape(8, 128, 128), GROUP)
    picked = call(pick_kernel, shape(1024, 128), [VMEM, VMEM])(ids, parts)
    picked = exchange(picked.reshape(512, 2, 128), LAYER + COLUMN).reshape(32, 16, 2, 128)
    return call(field_kernel, shape(8, 128, kind=F32), [VMEM, VMEM])(rows, picked).reshape(1024)


def solution(mesh):
    fine = Mesh(mesh.devices.reshape(4, 2, 4, 2, 8), ("x", "zh", "y", "c", "zl"))
    every = ("x", "zh", "y", "c", "zl")
    in_specs = (P(every, None, None), P(every), P("zl", None, None), P("zl", None))
    return jax.shard_map(body, mesh=fine, in_specs=in_specs, out_specs=P(every), check_vma=False)
```

```python
import functools

import jax
import jax.numpy as jnp
import numpy as np
from jax import lax
from jax.experimental import pallas as pl
from jax.experimental.pallas import tpu as pltpu
from jax.sharding import Mesh, PartitionSpec as P

GX = 8
GY = 32
CZS = 4
RUN = 128
BF = jnp.bfloat16
F32 = jnp.float32

COLUMN = ("zh", "zl")
LAYER = ("x", "y", "c")
SLABS = ("x", "zh", "zl")
GROUP = ("y", "c")
VMEM = pl.BlockSpec(memory_space=pltpu.VMEM)
SMEM = pl.BlockSpec(memory_space=pltpu.SMEM)


def iota(shape, dim):
    return lax.broadcasted_iota(jnp.int32, shape, dim)


def mask(where):
    return jnp.where(where, 1.0, 0.0)


def dot(a, b, dims=((1,), (0,)), precision=None):
    return lax.dot_general(a, b, (dims, ((), ())), precision=precision, preferred_element_type=F32)


def pack_kernel(offsets_ref, rows_ref, cells_ref, moments_ref):
    to, at = iota((64, 128), 0), iota((64, 128), 1)
    part = mask(at == 2 * to).astype(BF)
    for z in range(16):
        moments_ref[z, 0:32] = dot(part, rows_ref[128 * z : 128 * z + 128, :]).astype(BF).reshape(32, 2, 128)
    inside = jnp.bitwise_and(cells_ref[...], RUN - 1).astype(F32)
    lane = iota((1, 128), 1)
    shifts = jnp.zeros((1, 128), F32)
    for k in range(16):
        for j in range(3):
            shifts = jnp.where(lane == 3 * k + j, offsets_ref[j, k].astype(F32), shifts)
    rows = []
    for z in range(16):
        rows += [inside[z // 2 : z // 2 + 1], shifts]
    moments_ref[:, 32] = jnp.concatenate(rows, axis=0).astype(BF).reshape(16, 2, 128)


def regroup_kernel(got_ref, out_ref, offsets_ref):
    peer, layer = lax.axis_index("y") * 2 + lax.axis_index("c"), lax.axis_index("zl")
    quarter, half = lax.rem(peer, 4), lax.rem(layer, 2)
    reach = jnp.int32(0)
    for a in range(8):
        reach = jnp.where(peer == a, REACH[a] % 8, reach)
    shard = lax.rem(layer + reach, 8)
    for z in range(16):
        out_ref[:, z] = got_ref[z, 0:32]
    extra = got_ref[:, 32].reshape(32, 128)
    row, lane = iota((32, 128), 0), iota((32, 128), 1)
    take_row, take_lane = iota((64, 128), 0), iota((64, 128), 1)
    ids = jnp.zeros((64, 128), F32)
    for i in range(2):
        put = mask((row % 2 == 0) & (lane - 32 * quarter == row + i))
        take = mask((take_row % 2 == 0) & (take_lane == 64 * half + take_row + i))
        taken = dot(take.astype(BF), extra, ((1,), (1,)))
        ids = ids + dot(taken.astype(BF), put.astype(BF))
    out_ref[:, 16] = ids.astype(BF).reshape(32, 2, 128)
    out_ref[:, 17:24] = jnp.zeros((32, 7, 2, 128), BF)
    own = jnp.sum(mask(row == 2 * shard + 1) * extra.astype(F32), axis=0, keepdims=True)
    offsets_ref[...] = jnp.broadcast_to(own, (8, 128)).astype(jnp.int32)


def sum_kernel(got_ref, cells_ref, ids_ref):
    cell = iota((128, 128), 0)
    total = jnp.zeros((128, 128), F32)
    for four in range(8):
        blocks = [got_ref[4 * four + j] for j in range(4)]
        ids = sum(block[32:48].astype(F32) for block in blocks)[0:1]
        ids_ref[four : four + 1, :] = ids
        hot = mask(ids.astype(jnp.int32) == cell).astype(BF)
        total = total + dot(hot, jnp.concatenate([block[0:32] for block in blocks], axis=0))
    cells = total.astype(BF)
    for peer in range(cells_ref.shape[0]):
        cells_ref[peer] = cells


def m2l_kernel(offsets_ref, ops_ref, own_ref, low_ref, high_ref, out_ref, rows, shifted):
    shifted[:, :, 0:3] = jnp.zeros((6, 9, 3, GY, 128), BF)
    shifted[:, :, 11:13] = jnp.zeros((6, 9, 2, GY, 128), BF)
    rows[:, 0:8, :] = jnp.zeros((GX, 8, 128), F32)
    rows[:, 40:48, :] = jnp.zeros((GX, 8, 128), F32)
    for plane in range(9):
        ref, at = (low_ref, plane) if plane < 3 else (own_ref, plane - 3) if plane < 7 else (high_ref, plane - 7)
        rows[:, 8:40, :] = ref[at * 256 : (at + 1) * 256, :].astype(F32).reshape(GX, GY, 128)
        for dy in range(6):
            shifted[dy, plane, 3:11] = rows[:, 5 + dy : 37 + dy, :].astype(BF)
    ops = ops_ref[...].reshape(16 * 128, 128)
    for z in range(CZS):
        windows = []
        for k in range(16):
            dz, dx, dy = offsets_ref[0, 3 * k], offsets_ref[0, 3 * k + 1], offsets_ref[0, 3 * k + 2]
            window = shifted[dy + 3, dz + (3 + z), pl.ds(dx + 3, GX)]
            windows.append(window.reshape(GX * GY, 128))
        total = jnp.dot(jnp.concatenate(windows, axis=1), ops, preferred_element_type=F32)
        out_ref[z * 256 : (z + 1) * 256, :] = total.astype(BF)


def pick_kernel(ids_ref, parts_ref, out_ref):
    local = parts_ref[0].astype(F32)
    for peer in range(1, parts_ref.shape[0]):
        local = local + parts_ref[peer].astype(F32)
    local = local.astype(BF)
    cell = iota((128, 128), 0)
    for four in range(8):
        hot = mask(ids_ref[four : four + 1, :].astype(jnp.int32) == cell).astype(BF)
        out_ref[128 * four : 128 * four + 128, :] = dot(hot, local, ((0,), (0,))).astype(BF)


def field_kernel(rows_ref, picked_ref, out_ref):
    to, at = iota((128, 256), 0), iota((128, 256), 1)
    part = mask(at == 2 * to + 1).astype(BF)
    for k in range(8):
        basis = dot(part, rows_ref[256 * k : 256 * k + 256, :])
        picked = [picked_ref[:, 2 * k + j].reshape(64, 128) for j in range(2)]
        product = basis * jnp.concatenate(picked, axis=0).astype(F32)
        out_ref[k : k + 1, :] = jnp.sum(product, axis=1)[None] * (128 ** -0.5)


REACH = (0, 4, 1, -1, 2, -2, 3, -3)


def ops_moves():
    moves = []
    for z in range(16):
        for a in range(8):
            reach = -4 if REACH[a] == 4 and z % 2 else REACH[a]
            moves.append((spot((z + reach) % 16, a), spot(z, a)))
    return moves


def spot(z, a):
    return (z // 8 * 8 + a) * 8 + z % 8


def slab_spot(s):
    return s % 4 * 16 + s // 4


def call(kernel, out_shape, in_specs, scratch=()):
    many = isinstance(out_shape, list)
    return pl.pallas_call(
        kernel,
        out_shape=out_shape,
        in_specs=in_specs,
        out_specs=[VMEM] * len(out_shape) if many else VMEM,
        scratch_shapes=list(scratch),
        compiler_params=pltpu.CompilerParams(vmem_limit_bytes=40 * 1024 * 1024),
    )


def shape(*size, kind=BF):
    return jax.ShapeDtypeStruct(size, kind)


def exchange(array, axes):
    return lax.all_to_all(array, axes, split_axis=0, concat_axis=0, tiled=True)


def body(bead_data, bead_cell, m2l_ops, offsets):
    rows = bead_data.reshape(2048, 128)
    moments = call(pack_kernel, shape(16, 33, 2, 128), [SMEM, VMEM, VMEM])(
        offsets.T, rows, bead_cell.reshape(8, 128)
    )
    moments = exchange(moments.reshape(528, 2, 128), COLUMN)
    m2l_ops, moments = lax.optimization_barrier((m2l_ops, moments))
    moments, shifts = call(
        regroup_kernel, [shape(32, 24, 2, 128), shape(8, 128, kind=jnp.int32)], [VMEM]
    )(moments.reshape(16, 33, 2, 128))
    moments = exchange(moments.reshape(768, 2, 128), LAYER).reshape(32, 48, 128)
    ops = lax.ppermute(m2l_ops, ("zh", "y", "c", "zl"), ops_moves())
    cells, ids = call(sum_kernel, [shape(8, 128, 128), shape(8, 128, kind=F32)], [VMEM])(moments)
    slab = exchange(cells, GROUP).reshape(1024, 128)
    low = lax.ppermute(slab[256:], SLABS, [(slab_spot(i), slab_spot(i + 1)) for i in range(63)])
    high = lax.ppermute(slab[:512], SLABS, [(slab_spot(i + 1), slab_spot(i)) for i in range(63)])
    parts = call(
        m2l_kernel,
        shape(1024, 128),
        [SMEM, VMEM, VMEM, VMEM, VMEM],
        [pltpu.VMEM((GX, 48, 128), F32), pltpu.VMEM((6, 9, 13, GY, 128), BF)],
    )(shifts, ops, slab, low, high)
    parts = exchange(parts.reshape(8, 128, 128), GROUP)
    picked = call(pick_kernel, shape(1024, 128), [VMEM, VMEM])(ids, parts)
    picked = exchange(picked.reshape(512, 2, 128), LAYER + COLUMN).reshape(32, 16, 2, 128)
    return call(field_kernel, shape(8, 128, kind=F32), [VMEM, VMEM])(rows, picked).reshape(1024)


def solution(mesh):
    fine = Mesh(mesh.devices.reshape(4, 2, 4, 2, 8), ("x", "zh", "y", "c", "zl"))
    every = ("x", "zh", "y", "c", "zl")
    in_specs = (P(every, None, None), P(every), P("zl", None, None), P("zl", None))
    return jax.shard_map(body, mesh=fine, in_specs=in_specs, out_specs=P(every), check_vma=False)
```

```python
import functools

import jax
import jax.numpy as jnp
import numpy as np
from jax import lax
from jax.experimental import pallas as pl
from jax.experimental.pallas import tpu as pltpu
from jax.sharding import Mesh, PartitionSpec as P

GX = 8
GY = 32
CZS = 4
RUN = 128
BF = jnp.bfloat16
F32 = jnp.float32

COLUMN = ("zh", "zl")
LAYER = ("xh", "xl", "y", "c")
SLABS = ("xh", "xl", "zh", "zl")
GROUP = ("y", "c")
PAIR = ("xl", "y", "c")
VMEM = pl.BlockSpec(memory_space=pltpu.VMEM)
SMEM = pl.BlockSpec(memory_space=pltpu.SMEM)


def iota(shape, dim):
    return lax.broadcasted_iota(jnp.int32, shape, dim)


def mask(where):
    return jnp.where(where, 1.0, 0.0)


def dot(a, b, dims=((1,), (0,)), precision=None):
    return lax.dot_general(a, b, (dims, ((), ())), precision=precision, preferred_element_type=F32)


def pack_kernel(offsets_ref, rows_ref, cells_ref, moments_ref):
    to, at = iota((64, 128), 0), iota((64, 128), 1)
    part = mask(at == 2 * to).astype(BF)
    for z in range(16):
        moments_ref[z, 0:32] = dot(part, rows_ref[128 * z : 128 * z + 128, :]).astype(BF).reshape(32, 2, 128)
    inside = jnp.bitwise_and(cells_ref[...], RUN - 1).astype(F32)
    lane = iota((1, 128), 1)
    shifts = jnp.zeros((1, 128), F32)
    for k in range(16):
        for j in range(3):
            shifts = jnp.where(lane == 3 * k + j, offsets_ref[j, k].astype(F32), shifts)
    rows = []
    for z in range(16):
        rows += [inside[z // 2 : z // 2 + 1], shifts]
    moments_ref[:, 32] = jnp.concatenate(rows, axis=0).astype(BF).reshape(16, 2, 128)


def regroup_kernel(got_ref, out_ref, offsets_ref):
    peer, layer = lax.axis_index("y") * 2 + lax.axis_index("c"), lax.axis_index("zl")
    quarter, half = lax.rem(peer, 4), lax.rem(layer, 2)
    reach = jnp.int32(0)
    for a in range(8):
        reach = jnp.where(peer == a, REACH[a] % 8, reach)
    shard = lax.rem(layer + reach, 8)
    for z in range(16):
        out_ref[:, z] = got_ref[z, 0:32]
    extra = got_ref[:, 32].reshape(32, 128)
    row, lane = iota((32, 128), 0), iota((32, 128), 1)
    take_row, take_lane = iota((64, 128), 0), iota((64, 128), 1)
    ids = jnp.zeros((64, 128), F32)
    for i in range(2):
        put = mask((row % 2 == 0) & (lane - 32 * quarter == row + i))
        take = mask((take_row % 2 == 0) & (take_lane == 64 * half + take_row + i))
        taken = dot(take.astype(BF), extra, ((1,), (1,)))
        ids = ids + dot(taken.astype(BF), put.astype(BF))
    out_ref[:, 16] = ids.astype(BF).reshape(32, 2, 128)
    out_ref[:, 17:24] = jnp.zeros((32, 7, 2, 128), BF)
    own = jnp.sum(mask(row == 2 * shard + 1) * extra.astype(F32), axis=0, keepdims=True)
    offsets_ref[...] = jnp.broadcast_to(own, (8, 128)).astype(jnp.int32)


def sum_kernel(got_ref, cells_ref, ids_ref):
    cell = iota((128, 128), 0)
    total = jnp.zeros((128, 128), F32)
    for four in range(8):
        blocks = [got_ref[4 * four + j] for j in range(4)]
        ids = sum(block[32:48].astype(F32) for block in blocks)[0:1]
        ids_ref[four : four + 1, :] = ids
        hot = mask(ids.astype(jnp.int32) == cell).astype(BF)
        total = total + dot(hot, jnp.concatenate([block[0:32] for block in blocks], axis=0))
    cells = total.astype(BF)
    for peer in range(cells_ref.shape[0]):
        cells_ref[peer] = cells


def m2l_kernel(offsets_ref, ops_ref, pair_ref, edge_ref, out_ref, rows, shifted):
    second = lax.axis_index("xl")
    shifted[:, :, 0:3] = jnp.zeros((6, 9, 3, GY, 128), BF)
    shifted[:, :, 11:13] = jnp.zeros((6, 9, 2, GY, 128), BF)
    rows[:, 0:8, :] = jnp.zeros((GX, 8, 128), F32)
    rows[:, 40:48, :] = jnp.zeros((GX, 8, 128), F32)
    for plane in range(9):
        if plane < 3:
            values = jnp.where(second == 1, pair_ref[plane + 1], edge_ref[plane])
        elif plane < 7:
            values = pair_ref[plane - 3 + 4 * second]
        else:
            values = jnp.where(second == 1, edge_ref[plane - 7], pair_ref[plane - 3])
        rows[:, 8:40, :] = values.astype(F32).reshape(GX, GY, 128)
        for dy in range(6):
            shifted[dy, plane, 3:11] = rows[:, 5 + dy : 37 + dy, :].astype(BF)
    ops = ops_ref[...].reshape(16 * 128, 128)
    for z in range(CZS):
        windows = []
        for k in range(16):
            dz, dx, dy = offsets_ref[0, 3 * k], offsets_ref[0, 3 * k + 1], offsets_ref[0, 3 * k + 2]
            window = shifted[dy + 3, dz + (3 + z), pl.ds(dx + 3, GX)]
            windows.append(window.reshape(GX * GY, 128))
        total = jnp.dot(jnp.concatenate(windows, axis=1), ops, preferred_element_type=F32)
        out_ref[z * 256 : (z + 1) * 256, :] = total.astype(BF)


def pick_kernel(ids_ref, parts_ref, out_ref):
    local = parts_ref[0].astype(F32)
    for peer in range(1, parts_ref.shape[0]):
        local = local + parts_ref[peer].astype(F32)
    local = local.astype(BF)
    cell = iota((128, 128), 0)
    for four in range(8):
        hot = mask(ids_ref[four : four + 1, :].astype(jnp.int32) == cell).astype(BF)
        out_ref[128 * four : 128 * four + 128, :] = dot(hot, local, ((0,), (0,))).astype(BF)


def field_kernel(rows_ref, picked_ref, out_ref):
    to, at = iota((128, 256), 0), iota((128, 256), 1)
    part = mask(at == 2 * to + 1).astype(BF)
    for k in range(8):
        basis = dot(part, rows_ref[256 * k : 256 * k + 256, :])
        picked = [picked_ref[:, 2 * k + j].reshape(64, 128) for j in range(2)]
        product = basis * jnp.concatenate(picked, axis=0).astype(F32)
        out_ref[k : k + 1, :] = jnp.sum(product, axis=1)[None] * (128 ** -0.5)


REACH = (0, 4, 1, -1, 2, -2, 3, -3)


STEPS = ((0, 2, 1, -1, 1, -1, 1, -1), (0, 2, 0, 0, 1, -1, 2, -2))


def ops_moves(step):
    moves = []
    for z in range(16):
        for a in range(8):
            reach = -step[a] if REACH[a] == 4 and z % 2 else step[a]
            moves.append((spot((z + reach) % 16, a), spot(z, a)))
    return moves


def spot(z, a):
    return (z // 8 * 8 + a) * 8 + z % 8


def slab_spot(s):
    return s % 4 * 16 + s // 4


def call(kernel, out_shape, in_specs, scratch=()):
    many = isinstance(out_shape, list)
    return pl.pallas_call(
        kernel,
        out_shape=out_shape,
        in_specs=in_specs,
        out_specs=[VMEM] * len(out_shape) if many else VMEM,
        scratch_shapes=list(scratch),
        compiler_params=pltpu.CompilerParams(vmem_limit_bytes=40 * 1024 * 1024),
    )


def shape(*size, kind=BF):
    return jax.ShapeDtypeStruct(size, kind)


def exchange(array, axes):
    return lax.all_to_all(array, axes, split_axis=0, concat_axis=0, tiled=True)


def body(bead_data, bead_cell, m2l_ops, offsets):
    rows = bead_data.reshape(2048, 128)
    moments = call(pack_kernel, shape(16, 33, 2, 128), [SMEM, VMEM, VMEM])(
        offsets.T, rows, bead_cell.reshape(8, 128)
    )
    moments = exchange(moments.reshape(528, 2, 128), COLUMN)
    m2l_ops, moments = lax.optimization_barrier((m2l_ops, moments))
    moments, shifts = call(
        regroup_kernel, [shape(32, 24, 2, 128), shape(8, 128, kind=jnp.int32)], [VMEM]
    )(moments.reshape(16, 33, 2, 128))
    moments = exchange(moments.reshape(768, 2, 128), LAYER).reshape(32, 48, 128)
    ops = m2l_ops
    for step in STEPS:
        ops = lax.ppermute(ops, ("zh", "y", "c", "zl"), ops_moves(step))
    cells, ids = call(sum_kernel, [shape(16, 128, 128), shape(8, 128, kind=F32)], [VMEM])(moments)
    pair = exchange(cells, PAIR).reshape(8, 256, 128)
    edge = lax.dynamic_slice_in_dim(pair, 5 * lax.axis_index("xl"), 3, axis=0)
    swaps = [(i, i + 1) for i in range(1, 63, 2)]
    swaps = [(slab_spot(i), slab_spot(j)) for i, j in swaps + [(j, i) for i, j in swaps]]
    edge = lax.ppermute(edge, SLABS, swaps)
    parts = call(
        m2l_kernel,
        shape(1024, 128),
        [SMEM, VMEM, VMEM, VMEM],
        [pltpu.VMEM((GX, 48, 128), F32), pltpu.VMEM((6, 9, 13, GY, 128), BF)],
    )(shifts, ops, pair, edge)
    parts = exchange(parts.reshape(8, 128, 128), GROUP)
    picked = call(pick_kernel, shape(1024, 128), [VMEM, VMEM])(ids, parts)
    picked = exchange(picked.reshape(512, 2, 128), LAYER + COLUMN).reshape(32, 16, 2, 128)
    return call(field_kernel, shape(8, 128, kind=F32), [VMEM, VMEM])(rows, picked).reshape(1024)


def solution(mesh):
    fine = Mesh(mesh.devices.reshape(2, 2, 2, 4, 2, 8), ("xh", "xl", "zh", "y", "c", "zl"))
    every = ("xh", "xl", "zh", "y", "c", "zl")
    in_specs = (P(every, None, None), P(every), P("zl", None, None), P("zl", None))
    return jax.shard_map(body, mesh=fine, in_specs=in_specs, out_specs=P(every), check_vma=False)
```

```python
import functools

import jax
import jax.numpy as jnp
import numpy as np
from jax import lax
from jax.experimental import pallas as pl
from jax.experimental.pallas import tpu as pltpu
from jax.sharding import Mesh, PartitionSpec as P

GX = 8
GY = 32
CZS = 4
RUN = 128
BF = jnp.bfloat16
F32 = jnp.float32

COLUMN = ("zh", "zl")
LAYER = ("x", "y", "c")
GROUP = ("y", "c")
VMEM = pl.BlockSpec(memory_space=pltpu.VMEM)
SMEM = pl.BlockSpec(memory_space=pltpu.SMEM)


def iota(shape, dim):
    return lax.broadcasted_iota(jnp.int32, shape, dim)


def mask(where):
    return jnp.where(where, 1.0, 0.0)


def dot(a, b, dims=((1,), (0,)), precision=None):
    return lax.dot_general(a, b, (dims, ((), ())), precision=precision, preferred_element_type=F32)


def pack_kernel(offsets_ref, rows_ref, cells_ref, moments_ref):
    to, at = iota((64, 128), 0), iota((64, 128), 1)
    part = mask(at == 2 * to).astype(BF)
    for z in range(16):
        moments_ref[z, 0:32] = dot(part, rows_ref[128 * z : 128 * z + 128, :]).astype(BF).reshape(32, 2, 128)
    inside = jnp.bitwise_and(cells_ref[...], RUN - 1).astype(F32)
    lane = iota((1, 128), 1)
    shifts = jnp.zeros((1, 128), F32)
    for k in range(16):
        for j in range(3):
            shifts = jnp.where(lane == 3 * k + j, offsets_ref[j, k].astype(F32), shifts)
    rows = []
    for z in range(16):
        rows += [inside[z // 2 : z // 2 + 1], shifts]
    moments_ref[:, 32] = jnp.concatenate(rows, axis=0).astype(BF).reshape(16, 2, 128)


def regroup_kernel(got_ref, out_ref, offsets_ref):
    peer, layer = lax.axis_index("y") * 2 + lax.axis_index("c"), lax.axis_index("zl")
    quarter, half = lax.rem(peer, 4), lax.rem(layer, 2)
    reach = jnp.int32(0)
    for a in range(8):
        reach = jnp.where(peer == a, REACH[a] % 8, reach)
    shard = lax.rem(layer + reach, 8)
    for z in range(16):
        out_ref[:, z] = got_ref[z, 0:32]
    extra = got_ref[:, 32].reshape(32, 128)
    row, lane = iota((32, 128), 0), iota((32, 128), 1)
    take_row, take_lane = iota((64, 128), 0), iota((64, 128), 1)
    ids = jnp.zeros((64, 128), F32)
    for i in range(2):
        put = mask((row % 2 == 0) & (lane - 32 * quarter == row + i))
        take = mask((take_row % 2 == 0) & (take_lane == 64 * half + take_row + i))
        taken = dot(take.astype(BF), extra, ((1,), (1,)))
        ids = ids + dot(taken.astype(BF), put.astype(BF))
    out_ref[:, 16] = ids.astype(BF).reshape(32, 2, 128)
    out_ref[:, 17:24] = jnp.zeros((32, 7, 2, 128), BF)
    own = jnp.sum(mask(row == 2 * shard + 1) * extra.astype(F32), axis=0, keepdims=True)
    offsets_ref[...] = jnp.broadcast_to(own, (8, 128)).astype(jnp.int32)


def sum_kernel(got_ref, cells_ref, ids_ref):
    cell = iota((128, 128), 0)
    total = jnp.zeros((128, 128), F32)
    for four in range(8):
        blocks = [got_ref[4 * four + j] for j in range(4)]
        ids = sum(block[32:48].astype(F32) for block in blocks)[0:1]
        ids_ref[four : four + 1, :] = ids
        hot = mask(ids.astype(jnp.int32) == cell).astype(BF)
        total = total + dot(hot, jnp.concatenate([block[0:32] for block in blocks], axis=0))
    cells = total.astype(BF)
    for peer in range(cells_ref.shape[0]):
        cells_ref[peer] = cells


def edge_kernel(slab_ref, out_ref):
    first = 1 - lax.axis_index("c")
    for plane in range(3):
        out_ref[plane] = slab_ref[first + plane]


def m2l_kernel(offsets_ref, ops_ref, slab_ref, near_ref, far_ref, out_ref, rows, shifted):
    core = lax.axis_index("c")
    shifted[:, :, 0:3] = jnp.zeros((6, 9, 3, GY, 128), BF)
    shifted[:, :, 11:13] = jnp.zeros((6, 9, 2, GY, 128), BF)
    rows[:, 0:8, :] = jnp.zeros((GX, 8, 128), F32)
    rows[:, 40:48, :] = jnp.zeros((GX, 8, 128), F32)
    for plane in range(9):
        if plane < 3:
            values = jnp.where(core == 0, near_ref[plane], far_ref[plane])
        elif plane < 7:
            values = slab_ref[plane - 3]
        else:
            values = jnp.where(core == 0, far_ref[plane - 7], near_ref[plane - 7])
        rows[:, 8:40, :] = values.astype(F32).reshape(GX, GY, 128)
        for dy in range(6):
            shifted[dy, plane, 3:11] = rows[:, 5 + dy : 37 + dy, :].astype(BF)
    ops = ops_ref[...].reshape(16 * 128, 128)
    for z in range(CZS):
        windows = []
        for k in range(16):
            dz, dx, dy = offsets_ref[0, 3 * k], offsets_ref[0, 3 * k + 1], offsets_ref[0, 3 * k + 2]
            window = shifted[dy + 3, dz + (3 + z), pl.ds(dx + 3, GX)]
            windows.append(window.reshape(GX * GY, 128))
        total = jnp.dot(jnp.concatenate(windows, axis=1), ops, preferred_element_type=F32)
        out_ref[z * 256 : (z + 1) * 256, :] = total.astype(BF)


def pick_kernel(ids_ref, parts_ref, out_ref):
    local = parts_ref[0].astype(F32)
    for peer in range(1, parts_ref.shape[0]):
        local = local + parts_ref[peer].astype(F32)
    local = local.astype(BF)
    cell = iota((128, 128), 0)
    for four in range(8):
        hot = mask(ids_ref[four : four + 1, :].astype(jnp.int32) == cell).astype(BF)
        out_ref[128 * four : 128 * four + 128, :] = dot(hot, local, ((0,), (0,))).astype(BF)


def field_kernel(rows_ref, picked_ref, out_ref):
    to, at = iota((128, 256), 0), iota((128, 256), 1)
    part = mask(at == 2 * to + 1).astype(BF)
    for k in range(8):
        basis = dot(part, rows_ref[256 * k : 256 * k + 256, :])
        picked = [picked_ref[:, 2 * k + j].reshape(64, 128) for j in range(2)]
        product = basis * jnp.concatenate(picked, axis=0).astype(F32)
        out_ref[k : k + 1, :] = jnp.sum(product, axis=1)[None] * (128 ** -0.5)


REACH = (0, 4, 1, -1, 2, -2, 3, -3)


def ops_moves():
    moves = []
    for z in range(16):
        for a in range(8):
            reach = -4 if REACH[a] == 4 and z % 2 else REACH[a]
            moves.append((spot((z + reach) % 16, a), spot(z, a)))
    return moves


def spot(z, a):
    return (z // 8 * 8 + a) * 8 + z % 8


def halo_moves():
    def at(s, core):
        x, z = s % 4, s // 4
        return ((x * 2 + z // 8) * 2 + core) * 8 + z % 8

    return [(at(i + core, core), at(i + 1 - core, core)) for i in range(63) for core in range(2)]


def call(kernel, out_shape, in_specs, scratch=()):
    many = isinstance(out_shape, list)
    return pl.pallas_call(
        kernel,
        out_shape=out_shape,
        in_specs=in_specs,
        out_specs=[VMEM] * len(out_shape) if many else VMEM,
        scratch_shapes=list(scratch),
        compiler_params=pltpu.CompilerParams(vmem_limit_bytes=40 * 1024 * 1024),
    )


def shape(*size, kind=BF):
    return jax.ShapeDtypeStruct(size, kind)


def exchange(array, axes):
    return lax.all_to_all(array, axes, split_axis=0, concat_axis=0, tiled=True)


def body(bead_data, bead_cell, m2l_ops, offsets):
    rows = bead_data.reshape(2048, 128)
    moments = call(pack_kernel, shape(16, 33, 2, 128), [SMEM, VMEM, VMEM])(
        offsets.T, rows, bead_cell.reshape(8, 128)
    )
    moments = exchange(moments.reshape(528, 2, 128), COLUMN)
    m2l_ops, moments = lax.optimization_barrier((m2l_ops, moments))
    moments, shifts = call(
        regroup_kernel, [shape(32, 24, 2, 128), shape(8, 128, kind=jnp.int32)], [VMEM]
    )(moments.reshape(16, 33, 2, 128))
    moments = exchange(moments.reshape(768, 2, 128), LAYER).reshape(32, 48, 128)
    ops = lax.ppermute(m2l_ops, ("zh", "y", "c", "zl"), ops_moves())
    cells, ids = call(sum_kernel, [shape(8, 128, 128), shape(8, 128, kind=F32)], [VMEM])(moments)
    slab = exchange(cells, GROUP).reshape(4, 256, 128)
    near = call(edge_kernel, shape(3, 256, 128), [VMEM])(slab)
    near, ops = lax.optimization_barrier((near, ops))
    near = lax.ppermute(near, ("x", "zh", "c", "zl"), halo_moves())
    far = lax.ppermute(near, "c", [(0, 1), (1, 0)])
    parts = call(
        m2l_kernel,
        shape(1024, 128),
        [SMEM, VMEM, VMEM, VMEM, VMEM],
        [pltpu.VMEM((GX, 48, 128), F32), pltpu.VMEM((6, 9, 13, GY, 128), BF)],
    )(shifts, ops, slab, near, far)
    parts = exchange(parts.reshape(8, 128, 128), GROUP)
    picked = call(pick_kernel, shape(1024, 128), [VMEM, VMEM])(ids, parts)
    picked = exchange(picked.reshape(512, 2, 128), LAYER + COLUMN).reshape(32, 16, 2, 128)
    return call(field_kernel, shape(8, 128, kind=F32), [VMEM, VMEM])(rows, picked).reshape(1024)


def solution(mesh):
    fine = Mesh(mesh.devices.reshape(4, 2, 4, 2, 8), ("x", "zh", "y", "c", "zl"))
    every = ("x", "zh", "y", "c", "zl")
    in_specs = (P(every, None, None), P(every), P("zl", None, None), P("zl", None))
    return jax.shard_map(body, mesh=fine, in_specs=in_specs, out_specs=P(every), check_vma=False)
```

```python
import functools

import jax
import jax.numpy as jnp
import numpy as np
from jax import lax
from jax.experimental import pallas as pl
from jax.experimental.pallas import tpu as pltpu
from jax.sharding import Mesh, PartitionSpec as P

GX = 8
GY = 32
CZS = 4
RUN = 128
BF = jnp.bfloat16
F32 = jnp.float32

COLUMN = ("zh", "zl")
LAYER = ("x", "y", "c")
SLABS = ("x", "zh", "zl")
GROUP = ("y", "c")
VMEM = pl.BlockSpec(memory_space=pltpu.VMEM)
SMEM = pl.BlockSpec(memory_space=pltpu.SMEM)


def iota(shape, dim):
    return lax.broadcasted_iota(jnp.int32, shape, dim)


def mask(where):
    return jnp.where(where, 1.0, 0.0)


def dot(a, b, dims=((1,), (0,)), precision=None):
    return lax.dot_general(a, b, (dims, ((), ())), precision=precision, preferred_element_type=F32)


def pack_kernel(offsets_ref, rows_ref, cells_ref, moments_ref):
    to, at = iota((64, 128), 0), iota((64, 128), 1)
    part = mask(at == 2 * to).astype(BF)
    for z in range(16):
        moments_ref[z, 0:32] = dot(part, rows_ref[128 * z : 128 * z + 128, :]).astype(BF).reshape(32, 2, 128)
    inside = jnp.bitwise_and(cells_ref[...], RUN - 1).astype(F32)
    lane = iota((1, 128), 1)
    shifts = jnp.zeros((1, 128), F32)
    for k in range(16):
        for j in range(3):
            shifts = jnp.where(lane == 3 * k + j, offsets_ref[j, k].astype(F32), shifts)
    rows = []
    for z in range(16):
        rows += [inside[z // 2 : z // 2 + 1], shifts]
    moments_ref[:, 32] = jnp.concatenate(rows, axis=0).astype(BF).reshape(16, 2, 128)


def regroup_kernel(got_ref, out_ref, offsets_ref):
    peer, layer = lax.axis_index("y") * 2 + lax.axis_index("c"), lax.axis_index("zl")
    quarter, half = lax.rem(peer, 4), lax.rem(layer, 2)
    reach = jnp.int32(0)
    for a in range(8):
        reach = jnp.where(peer == a, REACH[a] % 8, reach)
    shard = lax.rem(layer + reach, 8)
    for z in range(16):
        out_ref[:, z] = got_ref[z, 0:32]
    extra = got_ref[:, 32].reshape(32, 128)
    row, lane = iota((32, 128), 0), iota((32, 128), 1)
    take_row, take_lane = iota((64, 128), 0), iota((64, 128), 1)
    ids = jnp.zeros((64, 128), F32)
    for i in range(2):
        put = mask((row % 2 == 0) & (lane - 32 * quarter == row + i))
        take = mask((take_row % 2 == 0) & (take_lane == 64 * half + take_row + i))
        taken = dot(take.astype(BF), extra, ((1,), (1,)))
        ids = ids + dot(taken.astype(BF), put.astype(BF))
    out_ref[:, 16] = ids.astype(BF).reshape(32, 2, 128)
    own = jnp.sum(mask(row == 2 * shard + 1) * extra.astype(F32), axis=0, keepdims=True)
    offsets_ref[...] = jnp.broadcast_to(own, (8, 128)).astype(jnp.int32)


def sum_kernel(got_ref, cells_ref, ids_ref):
    cell = iota((128, 128), 0)
    total = jnp.zeros((128, 128), F32)
    every = got_ref[:, 16].reshape(64, 128).astype(F32)
    for four in range(8):
        ids = jnp.sum(every[8 * four : 8 * four + 8], axis=0, keepdims=True)
        ids_ref[four : four + 1, :] = ids
        hot = mask(ids.astype(jnp.int32) == cell).astype(BF)
        total = total + dot(hot, got_ref[4 * four : 4 * four + 4, 0:16].reshape(128, 128))
    cells = total.astype(BF)
    for peer in range(cells_ref.shape[0]):
        cells_ref[peer] = cells


def m2l_kernel(offsets_ref, ops_ref, own_ref, low_ref, high_ref, out_ref, rows, shifted):
    shifted[:, :, 0:3] = jnp.zeros((6, 9, 3, GY, 128), BF)
    shifted[:, :, 11:13] = jnp.zeros((6, 9, 2, GY, 128), BF)
    rows[:, 0:8, :] = jnp.zeros((GX, 8, 128), F32)
    rows[:, 40:48, :] = jnp.zeros((GX, 8, 128), F32)
    for plane in range(9):
        ref, at = (low_ref, plane) if plane < 3 else (own_ref, plane - 3) if plane < 7 else (high_ref, plane - 7)
        rows[:, 8:40, :] = ref[at * 256 : (at + 1) * 256, :].astype(F32).reshape(GX, GY, 128)
        for dy in range(6):
            shifted[dy, plane, 3:11] = rows[:, 5 + dy : 37 + dy, :].astype(BF)
    ops = ops_ref[...].reshape(16 * 128, 128)
    for z in range(CZS):
        windows = []
        for k in range(16):
            dz, dx, dy = offsets_ref[0, 3 * k], offsets_ref[0, 3 * k + 1], offsets_ref[0, 3 * k + 2]
            window = shifted[dy + 3, dz + (3 + z), pl.ds(dx + 3, GX)]
            windows.append(window.reshape(GX * GY, 128))
        total = jnp.dot(jnp.concatenate(windows, axis=1), ops, preferred_element_type=F32)
        out_ref[z * 256 : (z + 1) * 256, :] = total.astype(BF)


def pick_kernel(ids_ref, parts_ref, out_ref):
    local = parts_ref[0].astype(F32)
    for peer in range(1, parts_ref.shape[0]):
        local = local + parts_ref[peer].astype(F32)
    local = local.astype(BF)
    cell = iota((128, 128), 0)
    for four in range(8):
        hot = mask(ids_ref[four : four + 1, :].astype(jnp.int32) == cell).astype(BF)
        out_ref[128 * four : 128 * four + 128, :] = dot(hot, local, ((0,), (0,))).astype(BF)


def basis_kernel(rows_ref, out_ref):
    to, at = iota((128, 256), 0), iota((128, 256), 1)
    part = mask(at == 2 * to + 1).astype(BF)
    for k in range(8):
        out_ref[128 * k : 128 * k + 128, :] = dot(part, rows_ref[256 * k : 256 * k + 256, :]).astype(BF)


def field_kernel(basis_ref, picked_ref, out_ref):
    for k in range(8):
        picked = [picked_ref[:, 2 * k + j].reshape(64, 128) for j in range(2)]
        basis = basis_ref[128 * k : 128 * k + 128, :].astype(F32)
        product = basis * jnp.concatenate(picked, axis=0).astype(F32)
        out_ref[k : k + 1, :] = jnp.sum(product, axis=1)[None] * (128 ** -0.5)


REACH = (0, 4, 1, -1, 2, -2, 3, -3)


def ops_moves():
    moves = []
    for z in range(16):
        for a in range(8):
            reach = -4 if REACH[a] == 4 and z % 2 else REACH[a]
            moves.append((spot((z + reach) % 16, a), spot(z, a)))
    return moves


def spot(z, a):
    return (z // 8 * 8 + a) * 8 + z % 8


def slab_spot(s):
    return s % 4 * 16 + s // 4


def call(kernel, out_shape, in_specs, scratch=(), cost=None):
    many = isinstance(out_shape, list)
    return pl.pallas_call(
        kernel,
        out_shape=out_shape,
        in_specs=in_specs,
        out_specs=[VMEM] * len(out_shape) if many else VMEM,
        scratch_shapes=list(scratch),
        compiler_params=pltpu.CompilerParams(vmem_limit_bytes=40 * 1024 * 1024),
        cost_estimate=cost and pl.CostEstimate(flops=cost, bytes_accessed=786432, transcendentals=0),
    )


def shape(*size, kind=BF):
    return jax.ShapeDtypeStruct(size, kind)


def exchange(array, axes):
    return lax.all_to_all(array, axes, split_axis=0, concat_axis=0, tiled=True)


def body(bead_data, bead_cell, m2l_ops, offsets):
    rows = bead_data.reshape(2048, 128)
    moments = call(pack_kernel, shape(16, 33, 2, 128), [SMEM, VMEM, VMEM])(
        offsets.T, rows, bead_cell.reshape(8, 128)
    )
    moments = exchange(moments.reshape(528, 2, 128), COLUMN)
    m2l_ops, moments = lax.optimization_barrier((m2l_ops, moments))
    moments, shifts = call(
        regroup_kernel, [shape(32, 17, 2, 128), shape(8, 128, kind=jnp.int32)], [VMEM]
    )(moments.reshape(16, 33, 2, 128))
    moments = exchange(moments.reshape(544, 2, 128), LAYER).reshape(32, 17, 2, 128)
    ops = lax.ppermute(m2l_ops, ("zh", "y", "c", "zl"), ops_moves())
    cells, ids = call(sum_kernel, [shape(8, 128, 128), shape(8, 128, kind=F32)], [VMEM])(moments)
    slab = exchange(cells, GROUP).reshape(1024, 128)
    low = lax.ppermute(slab[256:], SLABS, [(slab_spot(i), slab_spot(i + 1)) for i in range(63)])
    high = lax.ppermute(slab[:512], SLABS, [(slab_spot(i + 1), slab_spot(i)) for i in range(63)])
    basis = call(basis_kernel, shape(1024, 128), [VMEM], cost=67_000_000)(rows)
    ops, basis = lax.optimization_barrier((ops, basis))
    parts = call(
        m2l_kernel,
        shape(1024, 128),
        [SMEM, VMEM, VMEM, VMEM, VMEM],
        [pltpu.VMEM((GX, 48, 128), F32), pltpu.VMEM((6, 9, 13, GY, 128), BF)],
    )(shifts, ops, slab, low, high)
    parts = exchange(parts.reshape(8, 128, 128), GROUP)
    picked = call(pick_kernel, shape(1024, 128), [VMEM, VMEM])(ids, parts)
    picked = exchange(picked.reshape(512, 2, 128), LAYER + COLUMN).reshape(32, 16, 2, 128)
    return call(field_kernel, shape(8, 128, kind=F32), [VMEM, VMEM])(basis, picked).reshape(1024)


def solution(mesh):
    fine = Mesh(mesh.devices.reshape(4, 2, 4, 2, 8), ("x", "zh", "y", "c", "zl"))
    every = ("x", "zh", "y", "c", "zl")
    in_specs = (P(every, None, None), P(every), P("zl", None, None), P("zl", None))
    return jax.shard_map(body, mesh=fine, in_specs=in_specs, out_specs=P(every), check_vma=False)
```

```python
import functools

import jax
import jax.numpy as jnp
import numpy as np
from jax import lax
from jax.experimental import pallas as pl
from jax.experimental.pallas import tpu as pltpu
from jax.sharding import Mesh, PartitionSpec as P

GX = 8
GY = 32
CZS = 4
RUN = 128
BF = jnp.bfloat16
F32 = jnp.float32

COLUMN = ("zh", "zl")
LAYER = ("x", "y", "c")
SLABS = ("x", "zh", "zl")
GROUP = ("y", "c")
VMEM = pl.BlockSpec(memory_space=pltpu.VMEM)
SMEM = pl.BlockSpec(memory_space=pltpu.SMEM)


def iota(shape, dim):
    return lax.broadcasted_iota(jnp.int32, shape, dim)


def mask(where):
    return jnp.where(where, 1.0, 0.0)


def dot(a, b, dims=((1,), (0,)), precision=None):
    return lax.dot_general(a, b, (dims, ((), ())), precision=precision, preferred_element_type=F32)


def pack_kernel(offsets_ref, rows_ref, cells_ref, moments_ref):
    to, at = iota((64, 128), 0), iota((64, 128), 1)
    part = mask(at == 2 * to).astype(BF)
    for z in range(16):
        moments_ref[z, 0:32] = dot(part, rows_ref[128 * z : 128 * z + 128, :]).astype(BF).reshape(32, 2, 128)
    inside = jnp.bitwise_and(cells_ref[...], RUN - 1).astype(F32)
    lane = iota((1, 128), 1)
    shifts = jnp.zeros((1, 128), F32)
    for k in range(16):
        for j in range(3):
            shifts = jnp.where(lane == 3 * k + j, offsets_ref[j, k].astype(F32), shifts)
    rows = []
    for z in range(16):
        rows += [inside[z // 2 : z // 2 + 1], shifts]
    moments_ref[:, 32] = jnp.concatenate(rows, axis=0).astype(BF).reshape(16, 2, 128)


def regroup_kernel(got_ref, out_ref, offsets_ref):
    peer, layer = lax.axis_index("y") * 2 + lax.axis_index("c"), lax.axis_index("zl")
    quarter, half = lax.rem(peer, 4), lax.rem(layer, 2)
    reach = jnp.int32(0)
    for a in range(8):
        reach = jnp.where(peer == a, REACH[a] % 8, reach)
    shard = lax.rem(layer + reach, 8)
    for z in range(16):
        out_ref[:, z] = got_ref[z, 0:32]
    extra = got_ref[:, 32].reshape(32, 128)
    row, lane = iota((32, 128), 0), iota((32, 128), 1)
    take_row, take_lane = iota((64, 128), 0), iota((64, 128), 1)
    ids = jnp.zeros((64, 128), F32)
    for i in range(2):
        put = mask((row % 2 == 0) & (lane - 32 * quarter == row + i))
        take = mask((take_row % 2 == 0) & (take_lane == 64 * half + take_row + i))
        taken = dot(take.astype(BF), extra, ((1,), (1,)))
        ids = ids + dot(taken.astype(BF), put.astype(BF))
    out_ref[:, 16] = ids.astype(BF).reshape(32, 2, 128)
    own = jnp.sum(mask(row == 2 * shard + 1) * extra.astype(F32), axis=0, keepdims=True)
    offsets_ref[...] = jnp.broadcast_to(own, (8, 128)).astype(jnp.int32)


def sum_kernel(got_ref, cells_ref, ids_ref):
    cell = iota((128, 128), 0)
    total = jnp.zeros((128, 128), F32)
    every = got_ref[:, 16].reshape(64, 128).astype(F32)
    for four in range(8):
        ids = jnp.sum(every[8 * four : 8 * four + 8], axis=0, keepdims=True)
        ids_ref[four : four + 1, :] = ids
        hot = mask(ids.astype(jnp.int32) == cell).astype(BF)
        total = total + dot(hot, got_ref[4 * four : 4 * four + 4, 0:16].reshape(128, 128))
    cells = total.astype(BF)
    for peer in range(cells_ref.shape[0]):
        cells_ref[peer] = cells


def fill(rows, shifted, plane, values):
    rows[:, 8:40, :] = values.astype(F32).reshape(GX, GY, 128)
    for dy in range(6):
        shifted[dy, plane, 3:11] = rows[:, 5 + dy : 37 + dy, :].astype(BF)


def shift_kernel(own_ref, shifted, rows):
    shifted[:, :, 0:3] = jnp.zeros((6, 9, 3, GY, 128), BF)
    shifted[:, :, 11:13] = jnp.zeros((6, 9, 2, GY, 128), BF)
    rows[:, 0:8, :] = jnp.zeros((GX, 8, 128), F32)
    rows[:, 40:48, :] = jnp.zeros((GX, 8, 128), F32)
    for plane in range(CZS):
        fill(rows, shifted, plane + 3, own_ref[plane * 256 : (plane + 1) * 256, :])


def m2l_kernel(offsets_ref, ops_ref, low_ref, high_ref, given_ref, out_ref, shifted, rows):
    rows[:, 0:8, :] = jnp.zeros((GX, 8, 128), F32)
    rows[:, 40:48, :] = jnp.zeros((GX, 8, 128), F32)
    for plane in range(3):
        fill(rows, shifted, plane, low_ref[plane * 256 : (plane + 1) * 256, :])
    for plane in range(2):
        fill(rows, shifted, plane + 7, high_ref[plane * 256 : (plane + 1) * 256, :])
    ops = ops_ref[...].reshape(16 * 128, 128)
    for z in range(CZS):
        windows = []
        for k in range(16):
            dz, dx, dy = offsets_ref[0, 3 * k], offsets_ref[0, 3 * k + 1], offsets_ref[0, 3 * k + 2]
            window = shifted[dy + 3, dz + (3 + z), pl.ds(dx + 3, GX)]
            windows.append(window.reshape(GX * GY, 128))
        total = jnp.dot(jnp.concatenate(windows, axis=1), ops, preferred_element_type=F32)
        out_ref[z * 256 : (z + 1) * 256, :] = total.astype(BF)


def pick_kernel(ids_ref, parts_ref, out_ref):
    local = parts_ref[0].astype(F32)
    for peer in range(1, parts_ref.shape[0]):
        local = local + parts_ref[peer].astype(F32)
    local = local.astype(BF)
    cell = iota((128, 128), 0)
    for four in range(8):
        hot = mask(ids_ref[four : four + 1, :].astype(jnp.int32) == cell).astype(BF)
        out_ref[128 * four : 128 * four + 128, :] = dot(hot, local, ((0,), (0,))).astype(BF)


def basis_kernel(rows_ref, out_ref):
    to, at = iota((128, 256), 0), iota((128, 256), 1)
    part = mask(at == 2 * to + 1).astype(BF)
    for k in range(8):
        out_ref[128 * k : 128 * k + 128, :] = dot(part, rows_ref[256 * k : 256 * k + 256, :]).astype(BF)


def field_kernel(basis_ref, picked_ref, out_ref):
    for k in range(8):
        picked = [picked_ref[:, 2 * k + j].reshape(64, 128) for j in range(2)]
        basis = basis_ref[128 * k : 128 * k + 128, :].astype(F32)
        product = basis * jnp.concatenate(picked, axis=0).astype(F32)
        out_ref[k : k + 1, :] = jnp.sum(product, axis=1)[None] * (128 ** -0.5)


REACH = (0, 4, 1, -1, 2, -2, 3, -3)


def ops_moves():
    moves = []
    for z in range(16):
        for a in range(8):
            reach = -4 if REACH[a] == 4 and z % 2 else REACH[a]
            moves.append((spot((z + reach) % 16, a), spot(z, a)))
    return moves


def spot(z, a):
    return (z // 8 * 8 + a) * 8 + z % 8


def slab_spot(s):
    return s % 4 * 16 + s // 4


def call(kernel, out_shape, in_specs, scratch=(), cost=None, aliases={}):
    many = isinstance(out_shape, list)
    return pl.pallas_call(
        kernel,
        out_shape=out_shape,
        in_specs=in_specs,
        out_specs=[VMEM] * len(out_shape) if many else VMEM,
        scratch_shapes=list(scratch),
        input_output_aliases=aliases,
        compiler_params=pltpu.CompilerParams(vmem_limit_bytes=40 * 1024 * 1024),
        cost_estimate=cost and pl.CostEstimate(flops=cost, bytes_accessed=786432, transcendentals=0),
    )


def shape(*size, kind=BF):
    return jax.ShapeDtypeStruct(size, kind)


def exchange(array, axes):
    return lax.all_to_all(array, axes, split_axis=0, concat_axis=0, tiled=True)


def body(bead_data, bead_cell, m2l_ops, offsets):
    rows = bead_data.reshape(2048, 128)
    moments = call(pack_kernel, shape(16, 33, 2, 128), [SMEM, VMEM, VMEM])(
        offsets.T, rows, bead_cell.reshape(8, 128)
    )
    moments = exchange(moments.reshape(528, 2, 128), COLUMN)
    m2l_ops, moments = lax.optimization_barrier((m2l_ops, moments))
    moments, shifts = call(
        regroup_kernel, [shape(32, 17, 2, 128), shape(8, 128, kind=jnp.int32)], [VMEM]
    )(moments.reshape(16, 33, 2, 128))
    moments = exchange(moments.reshape(544, 2, 128), LAYER).reshape(32, 17, 2, 128)
    ops = lax.ppermute(m2l_ops, ("zh", "y", "c", "zl"), ops_moves())
    cells, ids = call(sum_kernel, [shape(8, 128, 128), shape(8, 128, kind=F32)], [VMEM])(moments)
    slab = exchange(cells, GROUP).reshape(1024, 128)
    low = lax.ppermute(slab[256:], SLABS, [(slab_spot(i), slab_spot(i + 1)) for i in range(63)])
    high = lax.ppermute(slab[:512], SLABS, [(slab_spot(i + 1), slab_spot(i)) for i in range(63)])
    basis = call(basis_kernel, shape(1024, 128), [VMEM], cost=67_000_000)(rows)
    ops, basis = lax.optimization_barrier((ops, basis))
    buffer = shape(6, 9, 13, GY, 128)
    rows = [pltpu.VMEM((GX, 48, 128), F32)]
    shifted = call(shift_kernel, buffer, [VMEM], rows, cost=100_000_000)(slab)
    parts, _ = call(
        m2l_kernel, [shape(1024, 128), buffer], [SMEM, VMEM, VMEM, VMEM, VMEM], rows, aliases={4: 1}
    )(shifts, ops, low, high, shifted)
    parts = exchange(parts.reshape(8, 128, 128), GROUP)
    picked = call(pick_kernel, shape(1024, 128), [VMEM, VMEM])(ids, parts)
    picked = exchange(picked.reshape(512, 2, 128), LAYER + COLUMN).reshape(32, 16, 2, 128)
    return call(field_kernel, shape(8, 128, kind=F32), [VMEM, VMEM])(basis, picked).reshape(1024)


def solution(mesh):
    fine = Mesh(mesh.devices.reshape(4, 2, 4, 2, 8), ("x", "zh", "y", "c", "zl"))
    every = ("x", "zh", "y", "c", "zl")
    in_specs = (P(every, None, None), P(every), P("zl", None, None), P("zl", None))
    return jax.shard_map(body, mesh=fine, in_specs=in_specs, out_specs=P(every), check_vma=False)
```

```python
import functools

import jax
import jax.numpy as jnp
import numpy as np
from jax import lax
from jax.experimental import pallas as pl
from jax.experimental.pallas import tpu as pltpu
from jax.sharding import Mesh, PartitionSpec as P

GX = 8
GY = 32
CZS = 4
RUN = 128
BF = jnp.bfloat16
F32 = jnp.float32

WIDE = ("zh", "zl", "x")
SLABS = ("x", "zh", "zl")
GROUP = ("y", "c")
VMEM = pl.BlockSpec(memory_space=pltpu.VMEM)
SMEM = pl.BlockSpec(memory_space=pltpu.SMEM)


def iota(shape, dim):
    return lax.broadcasted_iota(jnp.int32, shape, dim)


def mask(where):
    return jnp.where(where, 1.0, 0.0)


def dot(a, b, dims=((1,), (0,)), precision=None):
    return lax.dot_general(a, b, (dims, ((), ())), precision=precision, preferred_element_type=F32)


def pack_kernel(offsets_ref, rows_ref, cells_ref, moments_ref):
    to, at = iota((64, 128), 0), iota((64, 128), 1)
    part = mask(at == 2 * to).astype(BF)
    for z in range(16):
        moments = dot(part, rows_ref[128 * z : 128 * z + 128, :]).astype(BF)
        moments_ref[4 * z : 4 * z + 4, 0:8] = moments.reshape(4, 8, 2, 128)
    inside = jnp.bitwise_and(cells_ref[...], RUN - 1).astype(F32)
    lane = iota((1, 128), 1)
    shifts = jnp.zeros((1, 128), F32)
    for k in range(16):
        for j in range(3):
            shifts = jnp.where(lane == 3 * k + j, offsets_ref[j, k].astype(F32), shifts)
    row = iota((16, 128), 0)
    for k in range(8):
        pairs = jnp.where(row % 2 == 0, inside[k : k + 1], shifts).astype(BF)
        moments_ref[8 * k : 8 * k + 8, 8] = pairs.reshape(8, 2, 128)


def regroup_kernel(got_ref, out_ref, offsets_ref):
    layer = lax.axis_index("zl")
    peer = lax.axis_index("y") * 2 + lax.axis_index("c")
    seat = lax.rem(layer, 2) * 4 + lax.axis_index("x")
    reach = jnp.int32(0)
    for a in range(8):
        reach = jnp.where(peer == a, REACH[a] % 8, reach)
    shard = lax.rem(layer + reach, 8)
    for owner in range(8):
        out_ref[owner, 0:64] = got_ref[:, owner]
    extra = got_ref[:, 8].reshape(128, 128)
    row, lane = iota((128, 128), 0), iota((128, 128), 1)
    take_row, take_lane = iota((16, 128), 0), iota((16, 128), 1)
    ids = jnp.zeros((16, 128), F32)
    for i in range(2):
        put = mask((row % 2 == 0) & (lane == row + i))
        take = mask((take_row % 2 == 0) & (take_lane == 16 * seat + take_row + i))
        taken = dot(take.astype(BF), extra, ((1,), (1,)))
        ids = ids + dot(taken.astype(BF), put.astype(BF))
    out_ref[:, 64] = ids.astype(BF).reshape(8, 2, 128)
    own = jnp.sum(mask(row == 8 * shard + 1) * extra.astype(F32), axis=0, keepdims=True)
    offsets_ref[...] = jnp.broadcast_to(own, (8, 128)).astype(jnp.int32)


def sum_kernel(got_ref, cells_ref, ids_ref):
    cell = iota((128, 128), 0)
    total = jnp.zeros((128, 128), F32)
    every = got_ref[:, 64].reshape(16, 128).astype(F32)
    for peer in range(8):
        ids = jnp.sum(every[2 * peer : 2 * peer + 2], axis=0, keepdims=True)
        ids_ref[peer : peer + 1, :] = ids
        hot = mask(ids.astype(jnp.int32) == cell).astype(BF)
        total = total + dot(hot, got_ref[peer, 0:64].reshape(128, 128))
    cells = total.astype(BF)
    for peer in range(cells_ref.shape[0]):
        cells_ref[peer] = cells


def fill(rows, shifted, plane, values):
    rows[:, 8:40, :] = values.astype(F32).reshape(GX, GY, 128)
    for dy in range(6):
        shifted[dy, plane, 3:11] = rows[:, 5 + dy : 37 + dy, :].astype(BF)


def shift_kernel(own_ref, shifted, rows):
    shifted[:, :, 0:3] = jnp.zeros((6, 9, 3, GY, 128), BF)
    shifted[:, :, 11:13] = jnp.zeros((6, 9, 2, GY, 128), BF)
    rows[:, 0:8, :] = jnp.zeros((GX, 8, 128), F32)
    rows[:, 40:48, :] = jnp.zeros((GX, 8, 128), F32)
    for plane in range(CZS):
        fill(rows, shifted, plane + 3, own_ref[plane * 256 : (plane + 1) * 256, :])


def m2l_kernel(offsets_ref, ops_ref, low_ref, high_ref, given_ref, out_ref, shifted, rows):
    rows[:, 0:8, :] = jnp.zeros((GX, 8, 128), F32)
    rows[:, 40:48, :] = jnp.zeros((GX, 8, 128), F32)
    for plane in range(3):
        fill(rows, shifted, plane, low_ref[plane * 256 : (plane + 1) * 256, :])
    for plane in range(2):
        fill(rows, shifted, plane + 7, high_ref[plane * 256 : (plane + 1) * 256, :])
    ops = ops_ref[...].reshape(16 * 128, 128)
    for z in range(CZS):
        windows = []
        for k in range(16):
            dz, dx, dy = offsets_ref[0, 3 * k], offsets_ref[0, 3 * k + 1], offsets_ref[0, 3 * k + 2]
            window = shifted[dy + 3, dz + (3 + z), pl.ds(dx + 3, GX)]
            windows.append(window.reshape(GX * GY, 128))
        total = jnp.dot(jnp.concatenate(windows, axis=1), ops, preferred_element_type=F32)
        out_ref[z * 256 : (z + 1) * 256, :] = total.astype(BF)


def pick_kernel(ids_ref, parts_ref, out_ref):
    local = parts_ref[0].astype(F32)
    for peer in range(1, parts_ref.shape[0]):
        local = local + parts_ref[peer].astype(F32)
    local = local.astype(BF)
    cell = iota((128, 128), 0)
    for four in range(8):
        hot = mask(ids_ref[four : four + 1, :].astype(jnp.int32) == cell).astype(BF)
        out_ref[128 * four : 128 * four + 128, :] = dot(hot, local, ((0,), (0,))).astype(BF)


def basis_kernel(rows_ref, out_ref):
    to, at = iota((128, 256), 0), iota((128, 256), 1)
    part = mask(at == 2 * to + 1).astype(BF)
    for k in range(8):
        out_ref[128 * k : 128 * k + 128, :] = dot(part, rows_ref[256 * k : 256 * k + 256, :]).astype(BF)


def field_kernel(basis_ref, picked_ref, out_ref):
    for k in range(8):
        picked = [picked_ref[:, 8 * k + j].reshape(16, 128) for j in range(8)]
        basis = basis_ref[128 * k : 128 * k + 128, :].astype(F32)
        product = basis * jnp.concatenate(picked, axis=0).astype(F32)
        out_ref[k : k + 1, :] = jnp.sum(product, axis=1)[None] * (128 ** -0.5)


REACH = (0, 4, 1, -1, 2, -2, 3, -3)


def ops_moves():
    moves = []
    for z in range(16):
        for a in range(8):
            reach = -4 if REACH[a] == 4 and z % 2 else REACH[a]
            moves.append((spot((z + reach) % 16, a), spot(z, a)))
    return moves


def spot(z, a):
    return (z // 8 * 8 + a) * 8 + z % 8


def slab_spot(s):
    return s % 4 * 16 + s // 4


def call(kernel, out_shape, in_specs, scratch=(), cost=None, aliases={}):
    many = isinstance(out_shape, list)
    return pl.pallas_call(
        kernel,
        out_shape=out_shape,
        in_specs=in_specs,
        out_specs=[VMEM] * len(out_shape) if many else VMEM,
        scratch_shapes=list(scratch),
        input_output_aliases=aliases,
        compiler_params=pltpu.CompilerParams(vmem_limit_bytes=40 * 1024 * 1024),
        cost_estimate=cost and pl.CostEstimate(flops=cost, bytes_accessed=786432, transcendentals=0),
    )


def shape(*size, kind=BF):
    return jax.ShapeDtypeStruct(size, kind)


def exchange(array, axes):
    return lax.all_to_all(array, axes, split_axis=0, concat_axis=0, tiled=True)


def body(bead_data, bead_cell, m2l_ops, offsets):
    rows = bead_data.reshape(2048, 128)
    moments = call(pack_kernel, shape(64, 9, 2, 128), [SMEM, VMEM, VMEM])(
        offsets.T, rows, bead_cell.reshape(8, 128)
    )
    moments = exchange(moments.reshape(576, 2, 128), WIDE)
    m2l_ops, moments = lax.optimization_barrier((m2l_ops, moments))
    moments, shifts = call(
        regroup_kernel, [shape(8, 65, 2, 128), shape(8, 128, kind=jnp.int32)], [VMEM]
    )(moments.reshape(64, 9, 2, 128))
    moments = exchange(moments.reshape(520, 2, 128), GROUP).reshape(8, 65, 2, 128)
    ops = lax.ppermute(m2l_ops, ("zh", "y", "c", "zl"), ops_moves())
    cells, ids = call(sum_kernel, [shape(8, 128, 128), shape(8, 128, kind=F32)], [VMEM])(moments)
    slab = exchange(cells, GROUP).reshape(1024, 128)
    low = lax.ppermute(slab[256:], SLABS, [(slab_spot(i), slab_spot(i + 1)) for i in range(63)])
    high = lax.ppermute(slab[:512], SLABS, [(slab_spot(i + 1), slab_spot(i)) for i in range(63)])
    basis = call(basis_kernel, shape(1024, 128), [VMEM], cost=67_000_000)(rows)
    ops, basis = lax.optimization_barrier((ops, basis))
    buffer = shape(6, 9, 13, GY, 128)
    rows = [pltpu.VMEM((GX, 48, 128), F32)]
    shifted = call(shift_kernel, buffer, [VMEM], rows, cost=100_000_000)(slab)
    parts, _ = call(
        m2l_kernel, [shape(1024, 128), buffer], [SMEM, VMEM, VMEM, VMEM, VMEM], rows, aliases={4: 1}
    )(shifts, ops, low, high, shifted)
    parts = exchange(parts.reshape(8, 128, 128), GROUP)
    picked = call(pick_kernel, shape(1024, 128), [VMEM, VMEM])(ids, parts)
    picked = exchange(picked.reshape(512, 2, 128), GROUP + WIDE).reshape(8, 64, 2, 128)
    return call(field_kernel, shape(8, 128, kind=F32), [VMEM, VMEM])(basis, picked).reshape(1024)


def solution(mesh):
    fine = Mesh(mesh.devices.reshape(4, 2, 4, 2, 8), ("x", "zh", "y", "c", "zl"))
    every = ("x", "zh", "y", "c", "zl")
    in_specs = (P(every, None, None), P(every), P("zl", None, None), P("zl", None))
    return jax.shard_map(body, mesh=fine, in_specs=in_specs, out_specs=P(every), check_vma=False)
```

```python
import functools

import jax
import jax.numpy as jnp
import numpy as np
from jax import lax
from jax.experimental import pallas as pl
from jax.experimental.pallas import tpu as pltpu
from jax.sharding import Mesh, PartitionSpec as P

GX = 8
GY = 32
CZS = 4
RUN = 128
BF = jnp.bfloat16
F32 = jnp.float32

COLUMN = ("zh", "zl")
LAYER = ("x", "y", "c")
SLABS = ("x", "zh", "zl")
GROUP = ("y", "c")
VMEM = pl.BlockSpec(memory_space=pltpu.VMEM)
ANY = pl.BlockSpec(memory_space=pl.ANY)
SMEM = pl.BlockSpec(memory_space=pltpu.SMEM)


def iota(shape, dim):
    return lax.broadcasted_iota(jnp.int32, shape, dim)


def mask(where):
    return jnp.where(where, 1.0, 0.0)


def dot(a, b, dims=((1,), (0,)), precision=None):
    return lax.dot_general(a, b, (dims, ((), ())), precision=precision, preferred_element_type=F32)


def pack_kernel(offsets_hbm, rows_hbm, cells_hbm, out_hbm, offsets_ref, rows_ref, cells_ref, moments_ref, sems):
    halves = [pl.ds(0, 1024), pl.ds(1024, 1024)]
    copies = [pltpu.make_async_copy(rows_hbm.at[half], rows_ref.at[half], sems.at[i]) for i, half in enumerate(halves)]
    copies.append(pltpu.make_async_copy(cells_hbm, cells_ref, sems.at[2]))
    copies.append(pltpu.make_async_copy(offsets_hbm, offsets_ref, sems.at[3]))
    for copy in copies:
        copy.start()
    copies[2].wait()
    copies[3].wait()
    inside = jnp.bitwise_and(cells_ref[...], RUN - 1).astype(F32)
    lane = iota((1, 128), 1)
    shifts = jnp.zeros((1, 128), F32)
    for k in range(16):
        for j in range(3):
            shifts = jnp.where(lane == 3 * k + j, offsets_ref[j, k].astype(F32), shifts)
    rows = []
    for z in range(16):
        rows += [inside[z // 2 : z // 2 + 1], shifts]
    moments_ref[:, 32] = jnp.concatenate(rows, axis=0).astype(BF).reshape(16, 2, 128)
    to, at = iota((64, 128), 0), iota((64, 128), 1)
    part = mask(at == 2 * to).astype(BF)
    outs = [pl.ds(0, 8), pl.ds(8, 8)]
    outs = [pltpu.make_async_copy(moments_ref.at[half], out_hbm.at[half], sems.at[4 + i]) for i, half in enumerate(outs)]
    for half in range(2):
        copies[half].wait()
        for z in range(8 * half, 8 * half + 8):
            moments_ref[z, 0:32] = dot(part, rows_ref[128 * z : 128 * z + 128, :]).astype(BF).reshape(32, 2, 128)
        outs[half].start()
    for copy in outs:
        copy.wait()


def regroup_kernel(got_ref, out_ref, offsets_ref):
    peer, layer = lax.axis_index("y") * 2 + lax.axis_index("c"), lax.axis_index("zl")
    quarter, half = lax.rem(peer, 4), lax.rem(layer, 2)
    reach = jnp.int32(0)
    for a in range(8):
        reach = jnp.where(peer == a, REACH[a] % 8, reach)
    shard = lax.rem(layer + reach, 8)
    for z in range(16):
        out_ref[:, z] = got_ref[z, 0:32]
    extra = got_ref[:, 32].reshape(32, 128)
    row, lane = iota((32, 128), 0), iota((32, 128), 1)
    take_row, take_lane = iota((64, 128), 0), iota((64, 128), 1)
    ids = jnp.zeros((64, 128), F32)
    for i in range(2):
        put = mask((row % 2 == 0) & (lane - 32 * quarter == row + i))
        take = mask((take_row % 2 == 0) & (take_lane == 64 * half + take_row + i))
        taken = dot(take.astype(BF), extra, ((1,), (1,)))
        ids = ids + dot(taken.astype(BF), put.astype(BF))
    out_ref[:, 16] = ids.astype(BF).reshape(32, 2, 128)
    own = jnp.sum(mask(row == 2 * shard + 1) * extra.astype(F32), axis=0, keepdims=True)
    offsets_ref[...] = jnp.broadcast_to(own, (8, 128)).astype(jnp.int32)


def sum_kernel(got_ref, cells_ref, ids_ref):
    cell = iota((128, 128), 0)
    total = jnp.zeros((128, 128), F32)
    every = got_ref[:, 16].reshape(64, 128).astype(F32)
    for four in range(8):
        ids = jnp.sum(every[8 * four : 8 * four + 8], axis=0, keepdims=True)
        ids_ref[four : four + 1, :] = ids
        hot = mask(ids.astype(jnp.int32) == cell).astype(BF)
        total = total + dot(hot, got_ref[4 * four : 4 * four + 4, 0:16].reshape(128, 128))
    cells = total.astype(BF)
    for peer in range(cells_ref.shape[0]):
        cells_ref[peer] = cells


def fill(rows, shifted, plane, values):
    rows[:, 8:40, :] = values.astype(F32).reshape(GX, GY, 128)
    for dy in range(6):
        shifted[dy, plane, 3:11] = rows[:, 5 + dy : 37 + dy, :].astype(BF)


def shift_kernel(own_ref, shifted, rows):
    shifted[:, :, 0:3] = jnp.zeros((6, 9, 3, GY, 128), BF)
    shifted[:, :, 11:13] = jnp.zeros((6, 9, 2, GY, 128), BF)
    rows[:, 0:8, :] = jnp.zeros((GX, 8, 128), F32)
    rows[:, 40:48, :] = jnp.zeros((GX, 8, 128), F32)
    for plane in range(CZS):
        fill(rows, shifted, plane + 3, own_ref[plane * 256 : (plane + 1) * 256, :])


def m2l_kernel(offsets_ref, ops_ref, low_ref, high_ref, given_ref, out_ref, shifted, rows):
    rows[:, 0:8, :] = jnp.zeros((GX, 8, 128), F32)
    rows[:, 40:48, :] = jnp.zeros((GX, 8, 128), F32)
    for plane in range(3):
        fill(rows, shifted, plane, low_ref[plane * 256 : (plane + 1) * 256, :])
    for plane in range(2):
        fill(rows, shifted, plane + 7, high_ref[plane * 256 : (plane + 1) * 256, :])
    ops = ops_ref[...].reshape(16 * 128, 128)
    for z in range(CZS):
        windows = []
        for k in range(16):
            dz, dx, dy = offsets_ref[0, 3 * k], offsets_ref[0, 3 * k + 1], offsets_ref[0, 3 * k + 2]
            window = shifted[dy + 3, dz + (3 + z), pl.ds(dx + 3, GX)]
            windows.append(window.reshape(GX * GY, 128))
        total = jnp.dot(jnp.concatenate(windows, axis=1), ops, preferred_element_type=F32)
        out_ref[z * 256 : (z + 1) * 256, :] = total.astype(BF)


def pick_kernel(ids_ref, parts_ref, out_ref):
    local = parts_ref[0].astype(F32)
    for peer in range(1, parts_ref.shape[0]):
        local = local + parts_ref[peer].astype(F32)
    local = local.astype(BF)
    cell = iota((128, 128), 0)
    for four in range(8):
        hot = mask(ids_ref[four : four + 1, :].astype(jnp.int32) == cell).astype(BF)
        out_ref[128 * four : 128 * four + 128, :] = dot(hot, local, ((0,), (0,))).astype(BF)


def basis_kernel(rows_ref, out_ref):
    to, at = iota((128, 256), 0), iota((128, 256), 1)
    part = mask(at == 2 * to + 1).astype(BF)
    for k in range(8):
        out_ref[128 * k : 128 * k + 128, :] = dot(part, rows_ref[256 * k : 256 * k + 256, :]).astype(BF)


def field_kernel(basis_ref, picked_ref, out_ref):
    for k in range(8):
        picked = [picked_ref[:, 2 * k + j].reshape(64, 128) for j in range(2)]
        basis = basis_ref[128 * k : 128 * k + 128, :].astype(F32)
        product = basis * jnp.concatenate(picked, axis=0).astype(F32)
        out_ref[k : k + 1, :] = jnp.sum(product, axis=1)[None] * (128 ** -0.5)


REACH = (0, 4, 1, -1, 2, -2, 3, -3)


def ops_moves():
    moves = []
    for z in range(16):
        for a in range(8):
            reach = -4 if REACH[a] == 4 and z % 2 else REACH[a]
            moves.append((spot((z + reach) % 16, a), spot(z, a)))
    return moves


def spot(z, a):
    return (z // 8 * 8 + a) * 8 + z % 8


def slab_spot(s):
    return s % 4 * 16 + s // 4


def call(kernel, out_shape, in_specs, scratch=(), cost=None, aliases={}, vmem=40, out=VMEM):
    many = isinstance(out_shape, list)
    return pl.pallas_call(
        kernel,
        out_shape=out_shape,
        in_specs=in_specs,
        out_specs=[VMEM] * len(out_shape) if many else out,
        scratch_shapes=list(scratch),
        input_output_aliases=aliases,
        compiler_params=pltpu.CompilerParams(vmem_limit_bytes=vmem * 1024 * 1024),
        cost_estimate=cost and pl.CostEstimate(flops=cost, bytes_accessed=786432, transcendentals=0),
    )


def shape(*size, kind=BF):
    return jax.ShapeDtypeStruct(size, kind)


def exchange(array, axes):
    return lax.all_to_all(array, axes, split_axis=0, concat_axis=0, tiled=True)


def body(bead_data, bead_cell, m2l_ops, offsets):
    rows = bead_data.reshape(2048, 128)
    scratch = [pltpu.SMEM((3, 16), jnp.int32), pltpu.VMEM((2048, 128), BF), pltpu.VMEM((8, 128), jnp.int32)]
    scratch += [pltpu.VMEM((16, 33, 2, 128), BF), pltpu.SemaphoreType.DMA((6,))]
    moments = call(pack_kernel, shape(16, 33, 2, 128), [ANY, ANY, ANY], scratch, vmem=60, out=ANY)(
        offsets.T, rows, bead_cell.reshape(8, 128)
    )
    moments = exchange(moments.reshape(528, 2, 128), COLUMN)
    m2l_ops, moments = lax.optimization_barrier((m2l_ops, moments))
    moments, shifts = call(
        regroup_kernel, [shape(32, 17, 2, 128), shape(8, 128, kind=jnp.int32)], [VMEM]
    )(moments.reshape(16, 33, 2, 128))
    moments = exchange(moments.reshape(544, 2, 128), LAYER).reshape(32, 17, 2, 128)
    ops = lax.ppermute(m2l_ops, ("zh", "y", "c", "zl"), ops_moves())
    cells, ids = call(sum_kernel, [shape(8, 128, 128), shape(8, 128, kind=F32)], [VMEM])(moments)
    slab = exchange(cells, GROUP).reshape(1024, 128)
    low = lax.ppermute(slab[256:], SLABS, [(slab_spot(i), slab_spot(i + 1)) for i in range(63)])
    high = lax.ppermute(slab[:512], SLABS, [(slab_spot(i + 1), slab_spot(i)) for i in range(63)])
    basis = call(basis_kernel, shape(1024, 128), [VMEM], cost=67_000_000)(rows)
    ops, basis = lax.optimization_barrier((ops, basis))
    buffer = shape(6, 9, 13, GY, 128)
    rows = [pltpu.VMEM((GX, 48, 128), F32)]
    shifted = call(shift_kernel, buffer, [VMEM], rows, cost=100_000_000)(slab)
    parts, _ = call(
        m2l_kernel, [shape(1024, 128), buffer], [SMEM, VMEM, VMEM, VMEM, VMEM], rows, aliases={4: 1}
    )(shifts, ops, low, high, shifted)
    parts = exchange(parts.reshape(8, 128, 128), GROUP)
    picked = call(pick_kernel, shape(1024, 128), [VMEM, VMEM])(ids, parts)
    picked = exchange(picked.reshape(512, 2, 128), LAYER + COLUMN).reshape(32, 16, 2, 128)
    return call(field_kernel, shape(8, 128, kind=F32), [VMEM, VMEM])(basis, picked).reshape(1024)


def solution(mesh):
    fine = Mesh(mesh.devices.reshape(4, 2, 4, 2, 8), ("x", "zh", "y", "c", "zl"))
    every = ("x", "zh", "y", "c", "zl")
    in_specs = (P(every, None, None), P(every), P("zl", None, None), P("zl", None))
    return jax.shard_map(body, mesh=fine, in_specs=in_specs, out_specs=P(every), check_vma=False)
```

```python
import functools

import jax
import jax.numpy as jnp
import numpy as np
from jax import lax
from jax.experimental import pallas as pl
from jax.experimental.pallas import tpu as pltpu
from jax.sharding import Mesh, PartitionSpec as P

GX = 8
GY = 32
CZS = 4
RUN = 128
BF = jnp.bfloat16
F32 = jnp.float32

COLUMN = ("zh", "zl")
LAYER = ("x", "y", "c")
SLABS = ("x", "zh", "zl")
GROUP = ("y", "c")
VMEM = pl.BlockSpec(memory_space=pltpu.VMEM)
ANY = pl.BlockSpec(memory_space=pl.ANY)
SMEM = pl.BlockSpec(memory_space=pltpu.SMEM)


def iota(shape, dim):
    return lax.broadcasted_iota(jnp.int32, shape, dim)


def mask(where):
    return jnp.where(where, 1.0, 0.0)


def dot(a, b, dims=((1,), (0,)), precision=None):
    return lax.dot_general(a, b, (dims, ((), ())), precision=precision, preferred_element_type=F32)


def pack_kernel(offsets_hbm, rows_hbm, cells_hbm, out_hbm, offsets_ref, rows_ref, cells_ref, moments_ref, sems):
    halves = [pl.ds(0, 1024), pl.ds(1024, 1024)]
    copies = [pltpu.make_async_copy(rows_hbm.at[half], rows_ref.at[half], sems.at[i]) for i, half in enumerate(halves)]
    copies.append(pltpu.make_async_copy(cells_hbm, cells_ref, sems.at[2]))
    copies.append(pltpu.make_async_copy(offsets_hbm, offsets_ref, sems.at[3]))
    for copy in copies:
        copy.start()
    copies[2].wait()
    copies[3].wait()
    inside = jnp.bitwise_and(cells_ref[...], RUN - 1).astype(F32)
    lane = iota((1, 128), 1)
    shifts = jnp.zeros((1, 128), F32)
    for k in range(16):
        for j in range(3):
            shifts = jnp.where(lane == 3 * k + j, offsets_ref[j, k].astype(F32), shifts)
    rows = []
    for z in range(16):
        rows += [inside[z // 2 : z // 2 + 1], shifts]
    moments_ref[:, 32] = jnp.concatenate(rows, axis=0).astype(BF).reshape(16, 2, 128)
    to, at = iota((64, 128), 0), iota((64, 128), 1)
    part = mask(at == 2 * to).astype(BF)
    outs = [pl.ds(0, 8), pl.ds(8, 8)]
    outs = [pltpu.make_async_copy(moments_ref.at[half], out_hbm.at[half], sems.at[4 + i]) for i, half in enumerate(outs)]
    for half in range(2):
        copies[half].wait()
        for z in range(8 * half, 8 * half + 8):
            moments_ref[z, 0:32] = dot(part, rows_ref[128 * z : 128 * z + 128, :]).astype(BF).reshape(32, 2, 128)
        outs[half].start()
    for copy in outs:
        copy.wait()


def regroup_kernel(got_ref, out_hbm, offsets_ref, out_ref, sems):
    peer, layer = lax.axis_index("y") * 2 + lax.axis_index("c"), lax.axis_index("zl")
    quarter, half = lax.rem(peer, 4), lax.rem(layer, 2)
    reach = jnp.int32(0)
    for a in range(8):
        reach = jnp.where(peer == a, REACH[a] % 8, reach)
    shard = lax.rem(layer + reach, 8)
    for z in range(16):
        out_ref[:, z] = got_ref[z, 0:32]
    parts = [pl.ds(0, 16), pl.ds(16, 1)]
    copies = [pltpu.make_async_copy(out_ref.at[:, part], out_hbm.at[:, part], sems.at[i]) for i, part in enumerate(parts)]
    copies[0].start()
    extra = got_ref[:, 32].reshape(32, 128)
    row, lane = iota((32, 128), 0), iota((32, 128), 1)
    take_row, take_lane = iota((64, 128), 0), iota((64, 128), 1)
    ids = jnp.zeros((64, 128), F32)
    for i in range(2):
        put = mask((row % 2 == 0) & (lane - 32 * quarter == row + i))
        take = mask((take_row % 2 == 0) & (take_lane == 64 * half + take_row + i))
        taken = dot(take.astype(BF), extra, ((1,), (1,)))
        ids = ids + dot(taken.astype(BF), put.astype(BF))
    out_ref[:, 16] = ids.astype(BF).reshape(32, 2, 128)
    copies[1].start()
    own = jnp.sum(mask(row == 2 * shard + 1) * extra.astype(F32), axis=0, keepdims=True)
    offsets_ref[...] = jnp.broadcast_to(own, (8, 128)).astype(jnp.int32)
    for copy in copies:
        copy.wait()


def sum_kernel(got_ref, cells_ref, ids_ref):
    cell = iota((128, 128), 0)
    total = jnp.zeros((128, 128), F32)
    every = got_ref[:, 16].reshape(64, 128).astype(F32)
    for four in range(8):
        ids = jnp.sum(every[8 * four : 8 * four + 8], axis=0, keepdims=True)
        ids_ref[four : four + 1, :] = ids
        hot = mask(ids.astype(jnp.int32) == cell).astype(BF)
        total = total + dot(hot, got_ref[4 * four : 4 * four + 4, 0:16].reshape(128, 128))
    cells = total.astype(BF)
    for peer in range(cells_ref.shape[0]):
        cells_ref[peer] = cells


def fill(rows, shifted, plane, values):
    rows[:, 8:40, :] = values.astype(F32).reshape(GX, GY, 128)
    for dy in range(6):
        shifted[dy, plane, 3:11] = rows[:, 5 + dy : 37 + dy, :].astype(BF)


def shift_kernel(own_ref, shifted, rows):
    shifted[:, :, 0:3] = jnp.zeros((6, 9, 3, GY, 128), BF)
    shifted[:, :, 11:13] = jnp.zeros((6, 9, 2, GY, 128), BF)
    rows[:, 0:8, :] = jnp.zeros((GX, 8, 128), F32)
    rows[:, 40:48, :] = jnp.zeros((GX, 8, 128), F32)
    for plane in range(CZS):
        fill(rows, shifted, plane + 3, own_ref[plane * 256 : (plane + 1) * 256, :])


def m2l_kernel(offsets_ref, ops_ref, low_ref, high_ref, given_ref, out_ref, shifted, rows):
    rows[:, 0:8, :] = jnp.zeros((GX, 8, 128), F32)
    rows[:, 40:48, :] = jnp.zeros((GX, 8, 128), F32)
    for plane in range(3):
        fill(rows, shifted, plane, low_ref[plane * 256 : (plane + 1) * 256, :])
    for plane in range(2):
        fill(rows, shifted, plane + 7, high_ref[plane * 256 : (plane + 1) * 256, :])
    ops = ops_ref[...].reshape(16 * 128, 128)
    for z in range(CZS):
        windows = []
        for k in range(16):
            dz, dx, dy = offsets_ref[0, 3 * k], offsets_ref[0, 3 * k + 1], offsets_ref[0, 3 * k + 2]
            window = shifted[dy + 3, dz + (3 + z), pl.ds(dx + 3, GX)]
            windows.append(window.reshape(GX * GY, 128))
        total = jnp.dot(jnp.concatenate(windows, axis=1), ops, preferred_element_type=F32)
        out_ref[z * 256 : (z + 1) * 256, :] = total.astype(BF)


def pick_kernel(ids_ref, parts_ref, out_ref):
    local = parts_ref[0].astype(F32)
    for peer in range(1, parts_ref.shape[0]):
        local = local + parts_ref[peer].astype(F32)
    local = local.astype(BF)
    cell = iota((128, 128), 0)
    for four in range(8):
        hot = mask(ids_ref[four : four + 1, :].astype(jnp.int32) == cell).astype(BF)
        out_ref[128 * four : 128 * four + 128, :] = dot(hot, local, ((0,), (0,))).astype(BF)


def basis_kernel(rows_ref, out_ref):
    to, at = iota((128, 256), 0), iota((128, 256), 1)
    part = mask(at == 2 * to + 1).astype(BF)
    for k in range(8):
        out_ref[128 * k : 128 * k + 128, :] = dot(part, rows_ref[256 * k : 256 * k + 256, :]).astype(BF)


def field_kernel(basis_ref, picked_ref, out_ref):
    for k in range(8):
        picked = [picked_ref[:, 2 * k + j].reshape(64, 128) for j in range(2)]
        basis = basis_ref[128 * k : 128 * k + 128, :].astype(F32)
        product = basis * jnp.concatenate(picked, axis=0).astype(F32)
        out_ref[k : k + 1, :] = jnp.sum(product, axis=1)[None] * (128 ** -0.5)


REACH = (0, 4, 1, -1, 2, -2, 3, -3)


def ops_moves():
    moves = []
    for z in range(16):
        for a in range(8):
            reach = -4 if REACH[a] == 4 and z % 2 else REACH[a]
            moves.append((spot((z + reach) % 16, a), spot(z, a)))
    return moves


def spot(z, a):
    return (z // 8 * 8 + a) * 8 + z % 8


def slab_spot(s):
    return s % 4 * 16 + s // 4


def call(kernel, out_shape, in_specs, scratch=(), cost=None, aliases={}, vmem=40, out=VMEM):
    many = isinstance(out_shape, list)
    return pl.pallas_call(
        kernel,
        out_shape=out_shape,
        in_specs=in_specs,
        out_specs=[VMEM] * len(out_shape) if many and out is VMEM else out,
        scratch_shapes=list(scratch),
        input_output_aliases=aliases,
        compiler_params=pltpu.CompilerParams(vmem_limit_bytes=vmem * 1024 * 1024),
        cost_estimate=cost and pl.CostEstimate(flops=cost, bytes_accessed=786432, transcendentals=0),
    )


def shape(*size, kind=BF):
    return jax.ShapeDtypeStruct(size, kind)


def exchange(array, axes):
    return lax.all_to_all(array, axes, split_axis=0, concat_axis=0, tiled=True)


def body(bead_data, bead_cell, m2l_ops, offsets):
    rows = bead_data.reshape(2048, 128)
    scratch = [pltpu.SMEM((3, 16), jnp.int32), pltpu.VMEM((2048, 128), BF), pltpu.VMEM((8, 128), jnp.int32)]
    scratch += [pltpu.VMEM((16, 33, 2, 128), BF), pltpu.SemaphoreType.DMA((6,))]
    moments = call(pack_kernel, shape(16, 33, 2, 128), [ANY, ANY, ANY], scratch, vmem=60, out=ANY)(
        offsets.T, rows, bead_cell.reshape(8, 128)
    )
    moments = exchange(moments.reshape(528, 2, 128), COLUMN)
    m2l_ops, moments = lax.optimization_barrier((m2l_ops, moments))
    moments, shifts = call(
        regroup_kernel,
        [shape(32, 17, 2, 128), shape(8, 128, kind=jnp.int32)],
        [VMEM],
        [pltpu.VMEM((32, 17, 2, 128), BF), pltpu.SemaphoreType.DMA((2,))],
        out=[ANY, VMEM],
    )(moments.reshape(16, 33, 2, 128))
    moments = exchange(moments.reshape(544, 2, 128), LAYER).reshape(32, 17, 2, 128)
    ops = lax.ppermute(m2l_ops, ("zh", "y", "c", "zl"), ops_moves())
    cells, ids = call(sum_kernel, [shape(8, 128, 128), shape(8, 128, kind=F32)], [VMEM])(moments)
    slab = exchange(cells, GROUP).reshape(1024, 128)
    low = lax.ppermute(slab[256:], SLABS, [(slab_spot(i), slab_spot(i + 1)) for i in range(63)])
    high = lax.ppermute(slab[:512], SLABS, [(slab_spot(i + 1), slab_spot(i)) for i in range(63)])
    basis = call(basis_kernel, shape(1024, 128), [VMEM], cost=67_000_000)(rows)
    ops, basis = lax.optimization_barrier((ops, basis))
    buffer = shape(6, 9, 13, GY, 128)
    rows = [pltpu.VMEM((GX, 48, 128), F32)]
    shifted = call(shift_kernel, buffer, [VMEM], rows, cost=100_000_000)(slab)
    parts, _ = call(
        m2l_kernel, [shape(1024, 128), buffer], [SMEM, VMEM, VMEM, VMEM, VMEM], rows, aliases={4: 1}
    )(shifts, ops, low, high, shifted)
    parts = exchange(parts.reshape(8, 128, 128), GROUP)
    picked = call(pick_kernel, shape(1024, 128), [VMEM, VMEM])(ids, parts)
    picked = exchange(picked.reshape(512, 2, 128), LAYER + COLUMN).reshape(32, 16, 2, 128)
    return call(field_kernel, shape(8, 128, kind=F32), [VMEM, VMEM])(basis, picked).reshape(1024)


def solution(mesh):
    fine = Mesh(mesh.devices.reshape(4, 2, 4, 2, 8), ("x", "zh", "y", "c", "zl"))
    every = ("x", "zh", "y", "c", "zl")
    in_specs = (P(every, None, None), P(every), P("zl", None, None), P("zl", None))
    return jax.shard_map(body, mesh=fine, in_specs=in_specs, out_specs=P(every), check_vma=False)
```

```python
import functools

import jax
import jax.numpy as jnp
import numpy as np
from jax import lax
from jax.experimental import pallas as pl
from jax.experimental.pallas import tpu as pltpu
from jax.sharding import Mesh, PartitionSpec as P

GX = 8
GY = 32
CZS = 4
RUN = 128
BF = jnp.bfloat16
F32 = jnp.float32

COLUMN = ("zh", "zl")
LAYER = ("x", "y", "c")
SLABS = ("x", "zh", "zl")
GROUP = ("y", "c")
VMEM = pl.BlockSpec(memory_space=pltpu.VMEM)
ANY = pl.BlockSpec(memory_space=pl.ANY)
SMEM = pl.BlockSpec(memory_space=pltpu.SMEM)


def iota(shape, dim):
    return lax.broadcasted_iota(jnp.int32, shape, dim)


def mask(where):
    return jnp.where(where, 1.0, 0.0)


def dot(a, b, dims=((1,), (0,)), precision=None):
    return lax.dot_general(a, b, (dims, ((), ())), precision=precision, preferred_element_type=F32)


def pack_kernel(offsets_hbm, rows_hbm, cells_hbm, out_hbm, offsets_ref, rows_ref, cells_ref, moments_ref, sems):
    halves = [pl.ds(0, 1024), pl.ds(1024, 1024)]
    copies = [pltpu.make_async_copy(rows_hbm.at[half], rows_ref.at[half], sems.at[i]) for i, half in enumerate(halves)]
    copies.append(pltpu.make_async_copy(cells_hbm, cells_ref, sems.at[2]))
    copies.append(pltpu.make_async_copy(offsets_hbm, offsets_ref, sems.at[3]))
    for copy in copies:
        copy.start()
    copies[2].wait()
    copies[3].wait()
    inside = jnp.bitwise_and(cells_ref[...], RUN - 1).astype(F32)
    lane = iota((1, 128), 1)
    shifts = jnp.zeros((1, 128), F32)
    for k in range(16):
        for j in range(3):
            shifts = jnp.where(lane == 3 * k + j, offsets_ref[j, k].astype(F32), shifts)
    rows = []
    for z in range(16):
        rows += [inside[z // 2 : z // 2 + 1], shifts]
    moments_ref[:, 32] = jnp.concatenate(rows, axis=0).astype(BF).reshape(16, 2, 128)
    to, at = iota((64, 128), 0), iota((64, 128), 1)
    part = mask(at == 2 * to).astype(BF)
    outs = [pl.ds(0, 8), pl.ds(8, 8)]
    outs = [pltpu.make_async_copy(moments_ref.at[half], out_hbm.at[half], sems.at[4 + i]) for i, half in enumerate(outs)]
    for half in range(2):
        copies[half].wait()
        for z in range(8 * half, 8 * half + 8):
            moments_ref[z, 0:32] = dot(part, rows_ref[128 * z : 128 * z + 128, :]).astype(BF).reshape(32, 2, 128)
        outs[half].start()
    for copy in outs:
        copy.wait()


def regroup_kernel(got_ref, out_ref, offsets_ref):
    peer, layer = lax.axis_index("y") * 2 + lax.axis_index("c"), lax.axis_index("zl")
    quarter, half = lax.rem(peer, 4), lax.rem(layer, 2)
    reach = jnp.int32(0)
    for a in range(8):
        reach = jnp.where(peer == a, REACH[a] % 8, reach)
    shard = lax.rem(layer + reach, 8)
    for z in range(16):
        out_ref[:, z] = got_ref[z, 0:32]
    extra = got_ref[:, 32].reshape(32, 128)
    row, lane = iota((32, 128), 0), iota((32, 128), 1)
    take_row, take_lane = iota((64, 128), 0), iota((64, 128), 1)
    ids = jnp.zeros((64, 128), F32)
    for i in range(2):
        put = mask((row % 2 == 0) & (lane - 32 * quarter == row + i))
        take = mask((take_row % 2 == 0) & (take_lane == 64 * half + take_row + i))
        taken = dot(take.astype(BF), extra, ((1,), (1,)))
        ids = ids + dot(taken.astype(BF), put.astype(BF))
    out_ref[:, 16] = ids.astype(BF).reshape(32, 2, 128)
    own = jnp.sum(mask(row == 2 * shard + 1) * extra.astype(F32), axis=0, keepdims=True)
    offsets_ref[...] = jnp.broadcast_to(own, (8, 128)).astype(jnp.int32)


def sum_kernel(got_ref, cells_ref, ids_ref):
    cell = iota((128, 128), 0)
    total = jnp.zeros((128, 128), F32)
    every = got_ref[:, 16].reshape(64, 128).astype(F32)
    for four in range(8):
        ids = jnp.sum(every[8 * four : 8 * four + 8], axis=0, keepdims=True)
        ids_ref[four : four + 1, :] = ids
        hot = mask(ids.astype(jnp.int32) == cell).astype(BF)
        total = total + dot(hot, got_ref[4 * four : 4 * four + 4, 0:16].reshape(128, 128))
    cells = total.astype(BF)
    for peer in range(cells_ref.shape[0]):
        cells_ref[peer] = cells


def fill(rows, shifted, plane, values):
    rows[:, 8:40, :] = values.astype(F32).reshape(GX, GY, 128)
    for dy in range(6):
        shifted[dy, plane, 3:11] = rows[:, 5 + dy : 37 + dy, :].astype(BF)


def shift_kernel(own_ref, shifted, rows):
    shifted[:, :, 0:3] = jnp.zeros((6, 9, 3, GY, 128), BF)
    shifted[:, :, 11:13] = jnp.zeros((6, 9, 2, GY, 128), BF)
    rows[:, 0:8, :] = jnp.zeros((GX, 8, 128), F32)
    rows[:, 40:48, :] = jnp.zeros((GX, 8, 128), F32)
    for plane in range(CZS):
        fill(rows, shifted, plane + 3, own_ref[plane * 256 : (plane + 1) * 256, :])


def m2l_kernel(shifts_ref, ops_ref, low_ref, high_ref, given_ref, out_ref, shifted, rows, offsets_ref, sem):
    copy = pltpu.make_async_copy(shifts_ref, offsets_ref, sem)
    copy.start()
    rows[:, 0:8, :] = jnp.zeros((GX, 8, 128), F32)
    rows[:, 40:48, :] = jnp.zeros((GX, 8, 128), F32)
    for plane in range(3):
        fill(rows, shifted, plane, low_ref[plane * 256 : (plane + 1) * 256, :])
    for plane in range(2):
        fill(rows, shifted, plane + 7, high_ref[plane * 256 : (plane + 1) * 256, :])
    copy.wait()
    ops = ops_ref[...].reshape(16 * 128, 128)
    for z in range(CZS):
        windows = []
        for k in range(16):
            dz, dx, dy = offsets_ref[0, 3 * k], offsets_ref[0, 3 * k + 1], offsets_ref[0, 3 * k + 2]
            window = shifted[dy + 3, dz + (3 + z), pl.ds(dx + 3, GX)]
            windows.append(window.reshape(GX * GY, 128))
        total = jnp.dot(jnp.concatenate(windows, axis=1), ops, preferred_element_type=F32)
        out_ref[z * 256 : (z + 1) * 256, :] = total.astype(BF)


def pick_kernel(ids_ref, parts_ref, out_ref):
    local = parts_ref[0].astype(F32)
    for peer in range(1, parts_ref.shape[0]):
        local = local + parts_ref[peer].astype(F32)
    local = local.astype(BF)
    cell = iota((128, 128), 0)
    for four in range(8):
        hot = mask(ids_ref[four : four + 1, :].astype(jnp.int32) == cell).astype(BF)
        out_ref[128 * four : 128 * four + 128, :] = dot(hot, local, ((0,), (0,))).astype(BF)


def basis_kernel(rows_ref, out_ref):
    to, at = iota((128, 256), 0), iota((128, 256), 1)
    part = mask(at == 2 * to + 1).astype(BF)
    for k in range(8):
        out_ref[128 * k : 128 * k + 128, :] = dot(part, rows_ref[256 * k : 256 * k + 256, :]).astype(BF)


def field_kernel(basis_ref, picked_ref, out_ref):
    for k in range(8):
        picked = [picked_ref[:, 2 * k + j].reshape(64, 128) for j in range(2)]
        basis = basis_ref[128 * k : 128 * k + 128, :].astype(F32)
        product = basis * jnp.concatenate(picked, axis=0).astype(F32)
        out_ref[k : k + 1, :] = jnp.sum(product, axis=1)[None] * (128 ** -0.5)


REACH = (0, 4, 1, -1, 2, -2, 3, -3)


def ops_moves():
    moves = []
    for z in range(16):
        for a in range(8):
            reach = -4 if REACH[a] == 4 and z % 2 else REACH[a]
            moves.append((spot((z + reach) % 16, a), spot(z, a)))
    return moves


def spot(z, a):
    return (z // 8 * 8 + a) * 8 + z % 8


def slab_spot(s):
    return s % 4 * 16 + s // 4


def call(kernel, out_shape, in_specs, scratch=(), cost=None, aliases={}, vmem=40, out=VMEM):
    many = isinstance(out_shape, list)
    return pl.pallas_call(
        kernel,
        out_shape=out_shape,
        in_specs=in_specs,
        out_specs=[VMEM] * len(out_shape) if many else out,
        scratch_shapes=list(scratch),
        input_output_aliases=aliases,
        compiler_params=pltpu.CompilerParams(vmem_limit_bytes=vmem * 1024 * 1024),
        cost_estimate=cost and pl.CostEstimate(flops=cost, bytes_accessed=786432, transcendentals=0),
    )


def shape(*size, kind=BF):
    return jax.ShapeDtypeStruct(size, kind)


def exchange(array, axes):
    return lax.all_to_all(array, axes, split_axis=0, concat_axis=0, tiled=True)


def body(bead_data, bead_cell, m2l_ops, offsets):
    rows = bead_data.reshape(2048, 128)
    scratch = [pltpu.SMEM((3, 16), jnp.int32), pltpu.VMEM((2048, 128), BF), pltpu.VMEM((8, 128), jnp.int32)]
    scratch += [pltpu.VMEM((16, 33, 2, 128), BF), pltpu.SemaphoreType.DMA((6,))]
    moments = call(pack_kernel, shape(16, 33, 2, 128), [ANY, ANY, ANY], scratch, vmem=60, out=ANY)(
        offsets.T, rows, bead_cell.reshape(8, 128)
    )
    moments = exchange(moments.reshape(528, 2, 128), COLUMN)
    m2l_ops, moments = lax.optimization_barrier((m2l_ops, moments))
    moments, shifts = call(
        regroup_kernel, [shape(32, 17, 2, 128), shape(8, 128, kind=jnp.int32)], [VMEM]
    )(moments.reshape(16, 33, 2, 128))
    moments = exchange(moments.reshape(544, 2, 128), LAYER).reshape(32, 17, 2, 128)
    ops = lax.ppermute(m2l_ops, ("zh", "y", "c", "zl"), ops_moves())
    cells, ids = call(sum_kernel, [shape(8, 128, 128), shape(8, 128, kind=F32)], [VMEM])(moments)
    slab = exchange(cells, GROUP).reshape(1024, 128)
    low = lax.ppermute(slab[256:], SLABS, [(slab_spot(i), slab_spot(i + 1)) for i in range(63)])
    high = lax.ppermute(slab[:512], SLABS, [(slab_spot(i + 1), slab_spot(i)) for i in range(63)])
    basis = call(basis_kernel, shape(1024, 128), [VMEM], cost=67_000_000)(rows)
    ops, basis = lax.optimization_barrier((ops, basis))
    buffer = shape(6, 9, 13, GY, 128)
    rows = [pltpu.VMEM((GX, 48, 128), F32)]
    shifted = call(shift_kernel, buffer, [VMEM], rows, cost=100_000_000)(slab)
    parts, _ = call(
        m2l_kernel,
        [shape(1024, 128), buffer],
        [VMEM] * 5,
        rows + [pltpu.SMEM((8, 128), jnp.int32), pltpu.SemaphoreType.DMA],
        aliases={4: 1},
    )(shifts, ops, low, high, shifted)
    parts = exchange(parts.reshape(8, 128, 128), GROUP)
    picked = call(pick_kernel, shape(1024, 128), [VMEM, VMEM])(ids, parts)
    picked = exchange(picked.reshape(512, 2, 128), LAYER + COLUMN).reshape(32, 16, 2, 128)
    return call(field_kernel, shape(8, 128, kind=F32), [VMEM, VMEM])(basis, picked).reshape(1024)


def solution(mesh):
    fine = Mesh(mesh.devices.reshape(4, 2, 4, 2, 8), ("x", "zh", "y", "c", "zl"))
    every = ("x", "zh", "y", "c", "zl")
    in_specs = (P(every, None, None), P(every), P("zl", None, None), P("zl", None))
    return jax.shard_map(body, mesh=fine, in_specs=in_specs, out_specs=P(every), check_vma=False)
```

```python
import functools

import jax
import jax.numpy as jnp
import numpy as np
from jax import lax
from jax.experimental import pallas as pl
from jax.experimental.pallas import tpu as pltpu
from jax.sharding import Mesh, PartitionSpec as P

GX = 8
GY = 32
CZS = 4
RUN = 128
BF = jnp.bfloat16
F32 = jnp.float32

COLUMN = ("zh", "zl")
LAYER = ("x", "y", "c")
SLABS = ("x", "zh", "zl")
GROUP = ("y", "c")
VMEM = pl.BlockSpec(memory_space=pltpu.VMEM)
ANY = pl.BlockSpec(memory_space=pl.ANY)
SMEM = pl.BlockSpec(memory_space=pltpu.SMEM)


def iota(shape, dim):
    return lax.broadcasted_iota(jnp.int32, shape, dim)


def mask(where):
    return jnp.where(where, 1.0, 0.0)


def dot(a, b, dims=((1,), (0,)), precision=None):
    return lax.dot_general(a, b, (dims, ((), ())), precision=precision, preferred_element_type=F32)


def pack_kernel(offsets_hbm, rows_hbm, cells_hbm, out_hbm, offsets_ref, rows_ref, cells_ref, moments_ref, sems):
    copies = [pltpu.make_async_copy(rows_hbm, rows_ref, sems.at[0])]
    copies.append(pltpu.make_async_copy(cells_hbm, cells_ref, sems.at[1]))
    copies.append(pltpu.make_async_copy(offsets_hbm, offsets_ref, sems.at[2]))
    for copy in copies:
        copy.start()
    copies[1].wait()
    copies[2].wait()
    inside = jnp.bitwise_and(cells_ref[...], RUN - 1).astype(F32)
    lane = iota((1, 128), 1)
    shifts = jnp.zeros((1, 128), F32)
    for k in range(16):
        for j in range(3):
            shifts = jnp.where(lane == 3 * k + j, offsets_ref[j, k].astype(F32), shifts)
    rows = []
    for z in range(16):
        rows += [inside[z // 2 : z // 2 + 1], shifts]
    moments_ref[:, 32] = jnp.concatenate(rows, axis=0).astype(BF).reshape(16, 2, 128)
    to, at = iota((64, 128), 0), iota((64, 128), 1)
    part = mask(at == 2 * to).astype(BF)
    outs = [pl.ds(0, 8), pl.ds(8, 8)]
    outs = [pltpu.make_async_copy(moments_ref.at[half], out_hbm.at[half], sems.at[3 + i]) for i, half in enumerate(outs)]
    copies[0].wait()
    for half in range(2):
        for z in range(8 * half, 8 * half + 8):
            moments_ref[z, 0:32] = dot(part, rows_ref[128 * z : 128 * z + 128, :]).astype(BF).reshape(32, 2, 128)
        outs[half].start()
    for copy in outs:
        copy.wait()


def regroup_kernel(got_ref, out_ref, offsets_ref):
    peer, layer = lax.axis_index("y") * 2 + lax.axis_index("c"), lax.axis_index("zl")
    quarter, half = lax.rem(peer, 4), lax.rem(layer, 2)
    reach = jnp.int32(0)
    for a in range(8):
        reach = jnp.where(peer == a, REACH[a] % 8, reach)
    shard = lax.rem(layer + reach, 8)
    for z in range(16):
        out_ref[:, z] = got_ref[z, 0:32]
    extra = got_ref[:, 32].reshape(32, 128)
    row, lane = iota((32, 128), 0), iota((32, 128), 1)
    take_row, take_lane = iota((64, 128), 0), iota((64, 128), 1)
    ids = jnp.zeros((64, 128), F32)
    for i in range(2):
        put = mask((row % 2 == 0) & (lane - 32 * quarter == row + i))
        take = mask((take_row % 2 == 0) & (take_lane == 64 * half + take_row + i))
        taken = dot(take.astype(BF), extra, ((1,), (1,)))
        ids = ids + dot(taken.astype(BF), put.astype(BF))
    out_ref[:, 16] = ids.astype(BF).reshape(32, 2, 128)
    own = jnp.sum(mask(row == 2 * shard + 1) * extra.astype(F32), axis=0, keepdims=True)
    offsets_ref[...] = jnp.broadcast_to(own, (8, 128)).astype(jnp.int32)


def sum_kernel(got_ref, cells_ref, ids_ref):
    cell = iota((128, 128), 0)
    total = jnp.zeros((128, 128), F32)
    every = got_ref[:, 16].reshape(64, 128).astype(F32)
    for four in range(8):
        ids = jnp.sum(every[8 * four : 8 * four + 8], axis=0, keepdims=True)
        ids_ref[four : four + 1, :] = ids
        hot = mask(ids.astype(jnp.int32) == cell).astype(BF)
        total = total + dot(hot, got_ref[4 * four : 4 * four + 4, 0:16].reshape(128, 128))
    cells = total.astype(BF)
    for peer in range(cells_ref.shape[0]):
        cells_ref[peer] = cells


def fill(rows, shifted, plane, values):
    rows[:, 8:40, :] = values.astype(F32).reshape(GX, GY, 128)
    for dy in range(6):
        shifted[dy, plane, 3:11] = rows[:, 5 + dy : 37 + dy, :].astype(BF)


def shift_kernel(own_ref, shifted, rows):
    shifted[:, :, 0:3] = jnp.zeros((6, 9, 3, GY, 128), BF)
    shifted[:, :, 11:13] = jnp.zeros((6, 9, 2, GY, 128), BF)
    rows[:, 0:8, :] = jnp.zeros((GX, 8, 128), F32)
    rows[:, 40:48, :] = jnp.zeros((GX, 8, 128), F32)
    for plane in range(CZS):
        fill(rows, shifted, plane + 3, own_ref[plane * 256 : (plane + 1) * 256, :])


def m2l_kernel(shifts_ref, ops_ref, low_ref, high_ref, given_ref, out_ref, shifted, rows, offsets_ref, sem):
    copy = pltpu.make_async_copy(shifts_ref, offsets_ref, sem)
    copy.start()
    rows[:, 0:8, :] = jnp.zeros((GX, 8, 128), F32)
    rows[:, 40:48, :] = jnp.zeros((GX, 8, 128), F32)
    for plane in range(3):
        fill(rows, shifted, plane, low_ref[plane * 256 : (plane + 1) * 256, :])
    for plane in range(2):
        fill(rows, shifted, plane + 7, high_ref[plane * 256 : (plane + 1) * 256, :])
    copy.wait()
    ops = ops_ref[...].reshape(16 * 128, 128)
    for z in range(CZS):
        windows = []
        for k in range(16):
            dz, dx, dy = offsets_ref[0, 3 * k], offsets_ref[0, 3 * k + 1], offsets_ref[0, 3 * k + 2]
            window = shifted[dy + 3, dz + (3 + z), pl.ds(dx + 3, GX)]
            windows.append(window.reshape(GX * GY, 128))
        total = jnp.dot(jnp.concatenate(windows, axis=1), ops, preferred_element_type=F32)
        out_ref[z * 256 : (z + 1) * 256, :] = total.astype(BF)


def pick_kernel(ids_ref, parts_ref, out_ref):
    local = parts_ref[0].astype(F32)
    for peer in range(1, parts_ref.shape[0]):
        local = local + parts_ref[peer].astype(F32)
    local = local.astype(BF)
    cell = iota((128, 128), 0)
    for four in range(8):
        hot = mask(ids_ref[four : four + 1, :].astype(jnp.int32) == cell).astype(BF)
        out_ref[128 * four : 128 * four + 128, :] = dot(hot, local, ((0,), (0,))).astype(BF)


def basis_kernel(rows_ref, out_ref):
    to, at = iota((128, 256), 0), iota((128, 256), 1)
    part = mask(at == 2 * to + 1).astype(BF)
    for k in range(8):
        out_ref[128 * k : 128 * k + 128, :] = dot(part, rows_ref[256 * k : 256 * k + 256, :]).astype(BF)


def field_kernel(basis_ref, picked_ref, out_ref):
    for k in range(8):
        picked = [picked_ref[:, 2 * k + j].reshape(64, 128) for j in range(2)]
        basis = basis_ref[128 * k : 128 * k + 128, :].astype(F32)
        product = basis * jnp.concatenate(picked, axis=0).astype(F32)
        out_ref[k : k + 1, :] = jnp.sum(product, axis=1)[None] * (128 ** -0.5)


REACH = (0, 4, 1, -1, 2, -2, 3, -3)


def ops_moves():
    moves = []
    for z in range(16):
        for a in range(8):
            reach = -4 if REACH[a] == 4 and z % 2 else REACH[a]
            moves.append((spot((z + reach) % 16, a), spot(z, a)))
    return moves


def spot(z, a):
    return (z // 8 * 8 + a) * 8 + z % 8


def slab_spot(s):
    return s % 4 * 16 + s // 4


def call(kernel, out_shape, in_specs, scratch=(), cost=None, aliases={}, vmem=40, out=VMEM):
    many = isinstance(out_shape, list)
    return pl.pallas_call(
        kernel,
        out_shape=out_shape,
        in_specs=in_specs,
        out_specs=[VMEM] * len(out_shape) if many else out,
        scratch_shapes=list(scratch),
        input_output_aliases=aliases,
        compiler_params=pltpu.CompilerParams(vmem_limit_bytes=vmem * 1024 * 1024),
        cost_estimate=cost and pl.CostEstimate(flops=cost, bytes_accessed=786432, transcendentals=0),
    )


def shape(*size, kind=BF):
    return jax.ShapeDtypeStruct(size, kind)


def exchange(array, axes):
    return lax.all_to_all(array, axes, split_axis=0, concat_axis=0, tiled=True)


def body(bead_data, bead_cell, m2l_ops, offsets):
    rows = bead_data.reshape(2048, 128)
    scratch = [pltpu.SMEM((3, 16), jnp.int32), pltpu.VMEM((2048, 128), BF), pltpu.VMEM((8, 128), jnp.int32)]
    scratch += [pltpu.VMEM((16, 33, 2, 128), BF), pltpu.SemaphoreType.DMA((5,))]
    moments = call(pack_kernel, shape(16, 33, 2, 128), [ANY, ANY, ANY], scratch, vmem=60, out=ANY)(
        offsets.T, rows, bead_cell.reshape(8, 128)
    )
    moments = exchange(moments.reshape(528, 2, 128), COLUMN)
    m2l_ops, moments = lax.optimization_barrier((m2l_ops, moments))
    moments, shifts = call(
        regroup_kernel, [shape(32, 17, 2, 128), shape(8, 128, kind=jnp.int32)], [VMEM]
    )(moments.reshape(16, 33, 2, 128))
    moments = exchange(moments.reshape(544, 2, 128), LAYER).reshape(32, 17, 2, 128)
    ops = lax.ppermute(m2l_ops, ("zh", "y", "c", "zl"), ops_moves())
    cells, ids = call(sum_kernel, [shape(8, 128, 128), shape(8, 128, kind=F32)], [VMEM])(moments)
    slab = exchange(cells, GROUP).reshape(1024, 128)
    low = lax.ppermute(slab[256:], SLABS, [(slab_spot(i), slab_spot(i + 1)) for i in range(63)])
    high = lax.ppermute(slab[:512], SLABS, [(slab_spot(i + 1), slab_spot(i)) for i in range(63)])
    basis = call(basis_kernel, shape(1024, 128), [VMEM], cost=67_000_000)(rows)
    ops, basis = lax.optimization_barrier((ops, basis))
    buffer = shape(6, 9, 13, GY, 128)
    rows = [pltpu.VMEM((GX, 48, 128), F32)]
    shifted = call(shift_kernel, buffer, [VMEM], rows, cost=100_000_000)(slab)
    parts, _ = call(
        m2l_kernel,
        [shape(1024, 128), buffer],
        [VMEM] * 5,
        rows + [pltpu.SMEM((8, 128), jnp.int32), pltpu.SemaphoreType.DMA],
        aliases={4: 1},
    )(shifts, ops, low, high, shifted)
    parts = exchange(parts.reshape(8, 128, 128), GROUP)
    picked = call(pick_kernel, shape(1024, 128), [VMEM, VMEM])(ids, parts)
    picked = exchange(picked.reshape(512, 2, 128), LAYER + COLUMN).reshape(32, 16, 2, 128)
    return call(field_kernel, shape(8, 128, kind=F32), [VMEM, VMEM])(basis, picked).reshape(1024)


def solution(mesh):
    fine = Mesh(mesh.devices.reshape(4, 2, 4, 2, 8), ("x", "zh", "y", "c", "zl"))
    every = ("x", "zh", "y", "c", "zl")
    in_specs = (P(every, None, None), P(every), P("zl", None, None), P("zl", None))
    return jax.shard_map(body, mesh=fine, in_specs=in_specs, out_specs=P(every), check_vma=False)
```
